512 devices in a mesh: strike: 8 (over x, core), dev: 64 (over z, y).
Axes of the slice: x: 4, y: 8, z: 8, core: 2. Of those that a mesh axis runs over, the one named last changes fastest.
Arguments:
- log_rate: float32 [32, 1024, 256], P(None, ('strike', 'dev')), may hold values from -1.5 to 1.5
- state_log: float32 [32, 1024, 256], P(None, ('strike', 'dev')), may hold values from -1 to 1
- a_coef: float32 [1024, 256], P(('strike', 'dev')), may hold values from 0.5 to 2
- b_coef: float32 [1024, 256], P(('strike', 'dev')), may hold values from 0.5 to 2
- near_src: int32 [512, 32], P(('strike', 'dev')), may hold values from 0 to 127, as said below
- near_dst: int32 [512, 32], P(('strike', 'dev')), may hold values from 0 to 1
- near_count: int32 [512], P(('strike', 'dev')), may hold values from 8 to 32, as said below
- near_blocks: bfloat16 [512, 32, 256, 256], P(('strike', 'dev')), may hold values from -0.1875 to 0.1875
- far_src: int32 [512, 32], P(('strike', 'dev')), may hold values from 0 to 127
- far_dst: int32 [512, 32], P(('strike', 'dev')), may hold values from 0 to 1
- far_coupling: float32 [512, 32, 32, 32], P(('strike', 'dev')), may hold values from -1 to 1
- cluster_bases: bfloat16 [1024, 32, 256], P(('strike', 'dev')), may hold values from -0.375 to 0.375
- transfer: float32 [1024, 32, 32], P(('strike', 'dev')), may hold values from -0.1875 to 0.1875
- coarse_coupling: float32 [1024, 8, 32, 32], P(('strike', 'dev')), may hold values from -0.625 to 0.625
Outputs:
- new_rate: float32 [32, 1024, 256], P(None, ('strike', 'dev'))
- new_state: float32 [32, 1024, 256], P(None, ('strike', 'dev'))
The draws below stay inside these ranges and needn't reach their ends.
Inputs may be any that keep to these rules, and one draw needn't show every extreme that they name: `near_src`: each near source cluster is owned by a device of the same strike group whose dev index differs from the holder's by at most 2. Only a device's first near_count slots are live; some device has all 32 slots live.
All inputs are finite; a program needn't handle non-finite values.
Results may differ from the reference program's by a relative error of at most 0.0045.
Values may be sent and summed in bfloat16 or wider, within the bound.
A program may use at most 64 MiB of HBM per device.

```python
import math
import jax
import jax.numpy as jnp
from jax import lax

P_SIZE = 256
R = 32
E = 32
CL = 2
NB = 32
NF = 32
REACH = 2
GROUP = 128
CLUSTERS = 1024
N_STRIKE = 8
N_DEV = 64
DEVICES = 512


def draw_near_src(key, part):
    key = jax.random.fold_in(key, 11)
    key_one, key_two = jax.random.split(key)
    dev_of = jnp.arange(DEVICES, dtype=jnp.int32) % N_DEV
    offset = jax.random.randint(key_one, (DEVICES, NB), -REACH, REACH + 1)
    target = dev_of[:, None] + offset
    target = jnp.where((target < 0) | (target >= N_DEV), dev_of[:, None] - offset, target)
    member = jax.random.randint(key_two, (DEVICES, NB), 0, CL)
    return (target * CL + member).astype(jnp.int32)


def draw_near_count(key, part):
    key = jax.random.fold_in(key, 12)
    key_one, key_two = jax.random.split(key)
    counts = jax.random.randint(key_one, (DEVICES,), NB // 4, NB + 1)
    full_dev = jax.random.randint(key_two, (), 0, DEVICES)
    return jnp.where(jnp.arange(DEVICES, dtype=jnp.int32) == full_dev, NB, counts).astype(jnp.int32)


def with_ends(drawn, key, least, top_value):
    spot = [jax.random.randint(jax.random.fold_in(key, axis), (), 0, length) for axis, length in enumerate(drawn.shape)]
    widest = drawn.shape.index(max(drawn.shape))
    beside = spot[:widest] + [(spot[widest] + 1) % drawn.shape[widest]] + spot[widest + 1:]
    return drawn.at[tuple(spot)].set(least).at[tuple(beside)].set(top_value)


def levels(rng, extent, pieces, least, high):
    level, own = 1.0, jax.random.fold_in(rng, 6)
    for axis_at, shards_of in pieces:
        draws = jnp.exp(jax.random.uniform(jax.random.fold_in(own, axis_at), (shards_of,), jnp.float32, least / len(pieces), high / len(pieces)))
        level = level * jnp.repeat(draws, extent[axis_at] // shards_of).reshape([-1 if axis == axis_at else 1 for axis in range(len(extent))])
    return level


def gaussian(key, shape, deviation, limit, shards=(), held_as=jnp.bfloat16):
    gain = levels(key, shape, shards, -0.22, 0.18) if shards else 1.0
    entries = jax.random.normal(key, shape, jnp.float32) * deviation * gain
    return jnp.minimum(jnp.maximum(entries, -limit), limit).astype(held_as)


def setup_inputs(seed: int = 0) -> dict:
    keys = jax.random.split(jax.random.key(seed), 15)
    return {
        "log_rate": jnp.clip(jax.random.uniform(keys[0], (E, CLUSTERS, P_SIZE), jnp.float32, -1.5, 1.5) * levels(keys[0], (E, CLUSTERS, P_SIZE), ((1, 512),), -0.4, 0.0), -1.5, 1.5),
        "state_log": jnp.clip(jax.random.uniform(keys[1], (E, CLUSTERS, P_SIZE), jnp.float32, -1.0, 1.0) * levels(keys[1], (E, CLUSTERS, P_SIZE), ((1, 512),), -0.4, 0.0), -1.0, 1.0),
        "a_coef": jnp.clip(jnp.exp(math.log(2.0) - 1.3862944 * jax.random.uniform(keys[2], (CLUSTERS, P_SIZE), jnp.float32) ** levels(keys[2], (CLUSTERS, P_SIZE), ((0, 512),), -0.2, 0.2)), 0.5, 2.0),
        "b_coef": jnp.clip(jnp.exp(math.log(2.0) - 1.3862944 * jax.random.uniform(keys[3], (CLUSTERS, P_SIZE), jnp.float32) ** levels(keys[3], (CLUSTERS, P_SIZE), ((0, 512),), -0.2, 0.2)), 0.5, 2.0),
        "near_src": draw_near_src(jax.random.fold_in(keys[14], 71), 0),
        "near_dst": with_ends(jax.random.randint(keys[5], (DEVICES, NB), 0, CL), jax.random.fold_in(keys[5], 1), 0, CL - 1).astype(jnp.int32),
        "near_count": draw_near_count(jax.random.fold_in(keys[14], 71), 0),
        "near_blocks": gaussian(keys[7], (DEVICES, NB, P_SIZE, P_SIZE), (4 * P_SIZE) ** -0.5, 0.1875, ((0, 512),)),
        "far_src": with_ends(jax.random.randint(keys[8], (DEVICES, NF), 0, GROUP), jax.random.fold_in(keys[8], 1), 0, GROUP - 1).astype(jnp.int32),
        "far_dst": with_ends(jax.random.randint(keys[9], (DEVICES, NF), 0, CL), jax.random.fold_in(keys[9], 1), 0, CL - 1).astype(jnp.int32),
        "far_coupling": gaussian(keys[10], (DEVICES, NF, R, R), R ** -0.5, 1.0, ((0, 512),), jnp.float32),
        "cluster_bases": gaussian(keys[11], (CLUSTERS, R, P_SIZE), P_SIZE ** -0.5, 0.375, ((0, 512),)),
        "transfer": gaussian(keys[12], (CLUSTERS, R, R), (R * CL * N_DEV // 4) ** -0.5, 0.1875, ((0, 512),), jnp.float32),
        "coarse_coupling": gaussian(keys[13], (CLUSTERS, N_STRIKE, R, R), (R * N_STRIKE // 3) ** -0.5, 0.625, ((0, 512),), jnp.float32),
    }


time_step = 0.25
viscous = 0.5
highest = lax.Precision.HIGHEST


def near_field(deficit, near_src, near_dst, near_count, near_blocks):
    slot_ids = jnp.arange(NB, dtype=jnp.int32)
    receivers = jnp.arange(CL, dtype=jnp.int32)

    def per_device(inputs):
        dev_index, sources, targets, live_count, blocks = inputs
        strike_group = dev_index // N_DEV
        src_rows = jnp.take(deficit, strike_group * GROUP + sources, axis=1).astype(jnp.float32)
        products = jnp.einsum('ekp,kpq->ekq', src_rows, blocks.astype(jnp.float32), precision=highest)
        live_mask = (slot_ids < live_count).astype(jnp.float32)
        receiver_pick = (targets[:, None] == receivers[None, :]).astype(jnp.float32) * live_mask[:, None]
        return jnp.einsum('ekq,kc->ceq', products, receiver_pick, precision=highest)

    gathered = lax.map(per_device, (jnp.arange(DEVICES, dtype=jnp.int32), near_src, near_dst, near_count, near_blocks))
    return jnp.transpose(gathered.reshape(CLUSTERS, E, P_SIZE), (1, 0, 2))


def far_sum(coefs, far_src, far_dst, far_coupling):
    receivers = jnp.arange(CL, dtype=jnp.int32)

    def per_device(inputs):
        dev_index, sources, targets, coupling = inputs
        strike_group = dev_index // N_DEV
        src_coefs = jnp.take(coefs, strike_group * GROUP + sources, axis=1)
        products = jnp.einsum('ekr,krs->eks', src_coefs, coupling, precision=highest)
        receiver_pick = (targets[:, None] == receivers[None, :]).astype(jnp.float32)
        return jnp.einsum('eks,kc->ces', products, receiver_pick, precision=highest)

    gathered = lax.map(per_device, (jnp.arange(DEVICES, dtype=jnp.int32), far_src, far_dst, far_coupling))
    return jnp.transpose(gathered.reshape(CLUSTERS, E, R), (1, 0, 2))


def slopes(rate_log, state_now, a_coef, b_coef, near_src, near_dst, near_count, near_blocks, far_src, far_dst, far_coupling, cluster_bases, transfer, coarse_coupling):
    velocity = jnp.exp(rate_log)
    deficit = (velocity - 1.0).astype(jnp.bfloat16)
    near = near_field(deficit, near_src, near_dst, near_count, near_blocks)
    bases_wide = cluster_bases.astype(jnp.float32)
    coefs = jnp.einsum('ecp,crp->ecr', deficit.astype(jnp.float32), bases_wide, precision=highest)
    shares = jnp.einsum('ecr,crs->ecs', coefs, transfer, precision=highest)
    group_coefs = jnp.sum(shares.reshape(E, N_STRIKE, GROUP, R), axis=2)
    coarse = jnp.einsum('ehr,chrs->ecs', group_coefs, coarse_coupling, precision=highest)
    expansion = (far_sum(coefs, far_src, far_dst, far_coupling) + coarse).astype(jnp.bfloat16)
    far = jnp.einsum('ecr,crp->ecp', expansion.astype(jnp.float32), bases_wide, precision=highest)
    stress_rate = -(near + far)
    state_change = jnp.exp(-state_now) - velocity
    rate_change = (stress_rate - b_coef[None] * state_change) / (a_coef[None] + viscous * velocity)
    return rate_change, state_change


def reference(log_rate, state_log, a_coef, b_coef, near_src, near_dst, near_count, near_blocks, far_src, far_dst, far_coupling, cluster_bases, transfer, coarse_coupling):
    def slope_at(rate_log, state_now):
        return slopes(rate_log, state_now, a_coef, b_coef, near_src, near_dst, near_count, near_blocks, far_src, far_dst, far_coupling, cluster_bases, transfer, coarse_coupling)

    first = slope_at(log_rate, state_log)
    second = slope_at(log_rate + 0.5 * time_step * first[0], state_log + 0.5 * time_step * first[1])
    third = slope_at(log_rate + 0.5 * time_step * second[0], state_log + 0.5 * time_step * second[1])
    fourth = slope_at(log_rate + time_step * third[0], state_log + time_step * third[1])
    new_rate = log_rate + (time_step / 6.0) * (first[0] + 2.0 * second[0] + 2.0 * third[0] + fourth[0])
    new_state = state_log + (time_step / 6.0) * (first[1] + 2.0 * second[1] + 2.0 * third[1] + fourth[1])
    return new_rate, new_state
```

```python
import jax
import jax.numpy as jnp
from jax import lax
from jax.experimental import pallas as pl
from jax.experimental.pallas import tpu as pltpu
from jax.sharding import PartitionSpec as P

CL = 2
NB = 32
NF = 32
REACH = 2
E = 32
R = 32
PS = 256
SIDE = 8
STAGES = 4
Q = 4
ROWS = R // Q

time_step = 0.25
viscous = 0.5
highest = lax.Precision.HIGHEST
f32 = jnp.float32
bf16 = jnp.bfloat16


def split(x):
    hi = lax.reduce_precision(x, 8, 7)
    return hi.astype(bf16), (x - hi).astype(bf16)


def pick_blocks(x, rows):
    block = lax.broadcasted_iota(jnp.int32, (rows, 128), 1) // E
    out = x[0:rows]
    for q in range(1, Q):
        out = jnp.where(block == q, x[q * rows : (q + 1) * rows], out)
    return out


def kernel(
    near_at,
    near_to,
    far_at,
    u_in,
    s_in,
    a_ref,
    b_ref,
    blocks_hbm,
    w1_ref,
    far_ref,
    coarse_ref,
    bases_ref,
    u_out,
    s_out,
    blocks,
    u_now,
    s_now,
    u_sum,
    s_sum,
    tab_a,
    tab_b,
    tab_p,
    tab_c,
    tab_n,
    work_n,
    work_b,
    x_far,
    load_sem,
    a_send,
    a_recv,
    b_send,
    b_recv,
    p_send,
    p_recv,
    c_send,
    c_recv,
    n_send,
    n_recv,
):
    st = lax.axis_index("strike")
    dv = lax.axis_index("dev")
    core = lax.rem(st, 2)
    z = lax.div(dv, SIDE)
    y = lax.rem(dv, SIDE)
    my_a = y + core * (z - y)
    my_b = z + core * (y - z)
    step_a = 1 + (SIDE - 1) * core
    step_b = SIDE - (SIDE - 1) * core

    def on_a(d):
        return (st, lax.rem(my_a + d, SIDE) * step_a + my_b * step_b)

    def on_b(d):
        return (st, my_a * step_a + lax.rem(my_b + d, SIDE) * step_b)

    def on_strike(d):
        return (lax.rem(st + d, SIDE), dv)

    offsets = [o for o in range(-REACH, REACH + 1) if o != 0]

    def has(o):
        return (dv + o >= 0) & (dv + o < SIDE * SIDE)

    load = pltpu.make_async_copy(blocks_hbm, blocks, load_sem)
    load.start()

    tab_n[...] = jnp.zeros_like(tab_n)

    barrier = pltpu.get_barrier_semaphore()
    for d in range(1, SIDE):
        for to in (on_a(d), on_b(d), on_strike(d)):
            pl.semaphore_signal(barrier, inc=1, device_id=to)
    n_near = jnp.int32(0)
    for o in offsets:
        n_near = n_near + has(o).astype(jnp.int32)

        @pl.when(has(o))
        def _():
            pl.semaphore_signal(barrier, inc=1, device_id=(st, dv + o))

    for c in range(CL):
        u_now[c] = u_in[c]
        s_now[c] = s_in[c]
    u_sum[...] = jnp.zeros_like(u_sum)
    s_sum[...] = jnp.zeros_like(s_sum)

    pl.semaphore_wait(barrier, 3 * (SIDE - 1) + n_near)

    def near_copy(s, o):
        slot = tab_n.at[s, pl.ds((REACH - o) * CL, CL)]
        return pltpu.make_async_remote_copy(
            src_ref=tab_n.at[s, pl.ds(REACH * CL, CL)],
            dst_ref=slot,
            send_sem=n_send.at[s, o + REACH],
            recv_sem=n_recv.at[s, REACH - o],
            device_id=(st, dv + o),
        )

    def send_all(ref, send, recv, to):
        for d in range(1, SIDE):
            pltpu.make_async_remote_copy(
                src_ref=ref, dst_ref=ref, send_sem=send, recv_sem=recv, device_id=to(d)
            ).start()

    def wait_bytes(ref, sem):
        part = ref.at[pl.ds(0, SIDE - 1)]
        pltpu.make_async_copy(part, part, sem).wait()

    def stage(s, carry):
        for c in range(CL):
            tab_n[s, REACH * CL + c] = (jnp.exp(u_now[c]) - 1.0).astype(bf16)
        outs = []
        for c in range(CL):
            deficit = tab_n[s, REACH * CL + c]
            wide = jnp.concatenate([deficit] * Q, axis=0)
            outs.append(
                lax.dot_general(
                    w1_ref[c], wide, (((1,), (1,)), ((), ())), preferred_element_type=f32
                )
            )
        coefs = jnp.concatenate([pick_blocks(o[0:R], ROWS) for o in outs], axis=0)
        share = outs[0][R : 2 * R] + outs[0][2 * R :] + outs[1][R : 2 * R] + outs[1][2 * R :]
        share = pick_blocks(share, ROWS)
        share_hi = share.astype(bf16).astype(f32)
        tab_a[s, my_a, 0 : 2 * ROWS] = coefs.astype(bf16)
        tab_a[s, my_a, 2 * ROWS : 4 * ROWS] = jnp.concatenate(
            [share_hi, share - share_hi], axis=0
        ).astype(bf16)
        send_all(tab_a.at[s, my_a], a_send.at[s], a_recv.at[s], on_a)
        for o in offsets:

            @pl.when(has(o))
            def _():
                near_copy(s, o).start()

        wait_bytes(tab_a.at[s], a_recv.at[s])
        total = jnp.zeros((2 * ROWS, 128), f32)
        for i in range(SIDE):
            total = total + tab_a[s, i, 2 * ROWS : 4 * ROWS].astype(f32)
        tab_p[s, my_b] = total[0:ROWS] + total[ROWS:]
        send_all(tab_p.at[s, my_b], p_send.at[s], p_recv.at[s], on_b)
        tab_b[s, my_b] = tab_a[s, :, 0 : 2 * ROWS]
        send_all(tab_b.at[s, my_b], b_send.at[s], b_recv.at[s], on_b)

        wait_bytes(tab_p.at[s], p_recv.at[s])
        group = jnp.sum(tab_p[s], axis=0)
        group_hi = group.astype(bf16).astype(f32)
        tab_c[s, st] = jnp.concatenate([group_hi, group - group_hi], axis=0).astype(bf16)
        send_all(tab_c.at[s, st], c_send.at[s], c_recv.at[s], on_strike)

        @pl.when(s == 0)
        def _():
            load.wait()

        for o in offsets:

            @pl.when(has(-o))
            def _():
                near_copy(s, o).wait_recv()

        work_n[...] = tab_n[s]
        near = jnp.zeros((CL * E, PS), f32)
        for k0 in range(0, NB, 4):
            lhs = []
            for k in range(k0, k0 + 4):
                rows = work_n[near_at[k]]
                lhs.append(
                    jnp.concatenate(
                        [rows * jnp.full((E, PS), near_to[c, k], f32).astype(bf16) for c in range(CL)],
                        axis=0,
                    )
                )
            near = near + jnp.dot(
                jnp.concatenate(lhs, axis=1),
                blocks[k0 : k0 + 4].reshape(4 * PS, PS),
                preferred_element_type=f32,
            )

        wait_bytes(tab_b.at[s], b_recv.at[s])
        work_b[...] = tab_b[s].reshape(SIDE * SIDE, 2 * ROWS, 128)
        for k in range(NF):
            x_far[k] = work_b[far_at[k]]
        out = jnp.dot(far_ref[...], x_far[...].reshape(NF * 2 * ROWS, 128), preferred_element_type=f32)
        wait_bytes(tab_c.at[s], c_recv.at[s])
        out = out + jnp.dot(
            coarse_ref[...], tab_c[s].reshape(SIDE * 2 * ROWS, 128), preferred_element_type=f32
        )
        flipped = pick_blocks(out, CL * R).T
        expansion = flipped[0:E] + flipped[E : 2 * E] + flipped[2 * E : 3 * E] + flipped[3 * E :]
        far = jnp.dot(expansion.astype(bf16), bases_ref[...], preferred_element_type=f32)

        weight = jnp.where((s == 1) | (s == 2), 2.0, 1.0).astype(f32)
        ahead = jnp.where(s == 2, time_step, 0.5 * time_step).astype(f32)
        for c in range(CL):
            velocity = jnp.exp(u_now[c])
            stress_rate = -(near[c * E : (c + 1) * E] + far[:, c * PS : (c + 1) * PS])
            ds = jnp.exp(-s_now[c]) - velocity
            du = (stress_rate - b_ref[c : c + 1] * ds) / (a_ref[c : c + 1] + viscous * velocity)
            u_sum[c] += weight * du
            s_sum[c] += weight * ds
            u_now[c] = u_in[c] + ahead * du
            s_now[c] = s_in[c] + ahead * ds

        wait_bytes(tab_a.at[s], a_send.at[s])
        wait_bytes(tab_p.at[s], p_send.at[s])
        wait_bytes(tab_b.at[s], b_send.at[s])
        wait_bytes(tab_c.at[s], c_send.at[s])
        for o in offsets:

            @pl.when(has(o))
            def _():
                near_copy(s, o).wait_send()

        return carry

    lax.fori_loop(0, STAGES, stage, 0)
    for c in range(CL):
        u_out[c] = u_in[c] + (time_step / 6.0) * u_sum[c]
        s_out[c] = s_in[c] + (time_step / 6.0) * s_sum[c]


def per_device(
    log_rate,
    state_log,
    a_coef,
    b_coef,
    near_src,
    near_dst,
    near_count,
    near_blocks,
    far_src,
    far_dst,
    far_coupling,
    cluster_bases,
    transfer,
    coarse_coupling,
):
    dv = lax.axis_index("dev")
    core = lax.axis_index("strike") % 2
    clusters = jnp.arange(CL, dtype=jnp.int32)

    near_at = (near_src[0] // CL - dv + REACH) * CL + near_src[0] % CL
    near_at = jnp.clip(near_at, 0, (2 * REACH + 1) * CL - 1)
    live = jnp.arange(NB, dtype=jnp.int32) < near_count[0]
    near_to = ((near_dst[0][None] == clusters[:, None]) & live[None]).astype(f32)
    owner = far_src[0] // CL
    far_at = jnp.where(core == 1, owner % SIDE * SIDE + owner // SIDE, owner)

    folded = jnp.einsum(
        "crs,crp->csp", transfer, cluster_bases.astype(f32), precision=highest
    )
    w1 = jnp.concatenate([cluster_bases, *split(folded)], axis=1)
    pick = (far_dst[0][:, None] == clusters)[:, :, None] & (far_src[0] % CL == clusters[:, None]).T[:, None, :]
    far_w = far_coupling[0].reshape(NF, Q, ROWS, R).transpose(1, 3, 0, 2)
    far_w = far_w[:, None, :, :, None, :] * pick.astype(f32).transpose(1, 0, 2)[None, :, None, :, :, None]
    far_w = far_w.reshape(Q * CL * R, NF * CL * ROWS).astype(bf16)
    coarse_w = coarse_coupling.reshape(CL, SIDE, Q, ROWS, R).transpose(2, 0, 4, 1, 3)
    coarse_w = jnp.broadcast_to(coarse_w[:, :, :, :, None], (Q, CL, R, SIDE, 2, ROWS))
    coarse_w = coarse_w.reshape(Q * CL * R, SIDE * 2 * ROWS).astype(bf16)
    bases = jnp.einsum("cd,crp->crdp", jnp.eye(CL, dtype=bf16), cluster_bases).reshape(CL * R, CL * PS)

    vmem = pl.BlockSpec(memory_space=pltpu.VMEM)
    smem = pl.BlockSpec(memory_space=pltpu.SMEM)
    state = (CL, E, PS)
    dma = pltpu.SemaphoreType.DMA
    u_new, s_new = pl.pallas_call(
        kernel,
        out_shape=[jax.ShapeDtypeStruct(state, f32)] * 2,
        in_specs=[smem, smem, smem, vmem, vmem, vmem, vmem, pl.BlockSpec(memory_space=pl.ANY)] + [vmem] * 4,
        out_specs=[vmem, vmem],
        scratch_shapes=[
            pltpu.VMEM((NB, PS, PS), bf16),
            pltpu.VMEM(state, f32),
            pltpu.VMEM(state, f32),
            pltpu.VMEM(state, f32),
            pltpu.VMEM(state, f32),
            pltpu.VMEM((STAGES, SIDE, 4 * ROWS, 128), bf16),
            pltpu.VMEM((STAGES, SIDE, SIDE, 2 * ROWS, 128), bf16),
            pltpu.VMEM((STAGES, SIDE, ROWS, 128), f32),
            pltpu.VMEM((STAGES, SIDE, 2 * ROWS, 128), bf16),
            pltpu.VMEM((STAGES, (2 * REACH + 1) * CL, E, PS), bf16),
            pltpu.VMEM(((2 * REACH + 1) * CL, E, PS), bf16),
            pltpu.VMEM((SIDE * SIDE, 2 * ROWS, 128), bf16),
            pltpu.VMEM((NF, 2 * ROWS, 128), bf16),
            dma,
            dma((STAGES,)),
            dma((STAGES,)),
            dma((STAGES,)),
            dma((STAGES,)),
            dma((STAGES,)),
            dma((STAGES,)),
            dma((STAGES,)),
            dma((STAGES,)),
            dma((STAGES, 2 * REACH + 1)),
            dma((STAGES, 2 * REACH + 1)),
        ],
        compiler_params=pltpu.CompilerParams(
            collective_id=0, has_side_effects=True, vmem_limit_bytes=32 * 1024 * 1024
        ),
    )(
        near_at,
        near_to,
        far_at,
        log_rate.transpose(1, 0, 2),
        state_log.transpose(1, 0, 2),
        a_coef,
        b_coef,
        near_blocks[0],
        w1,
        far_w,
        coarse_w,
        bases,
    )
    return u_new.transpose(1, 0, 2), s_new.transpose(1, 0, 2)


def solution(mesh):
    cluster = ("strike", "dev")
    state = P(None, cluster, None)
    placed = (
        state,
        state,
        P(cluster, None),
        P(cluster, None),
        P(cluster, None),
        P(cluster, None),
        P(cluster),
        P(cluster, None, None, None),
        P(cluster, None),
        P(cluster, None),
        P(cluster, None, None, None),
        P(cluster, None, None),
        P(cluster, None, None),
        P(cluster, None, None, None),
    )
    return jax.shard_map(
        per_device, mesh=mesh, in_specs=placed, out_specs=(state, state), check_vma=False
    )
```

```python
import jax
import jax.numpy as jnp
from jax import lax
from jax.experimental import pallas as pl
from jax.experimental.pallas import tpu as pltpu
from jax.sharding import PartitionSpec as P

CL = 2
NB = 32
NF = 32
REACH = 2
E = 32
R = 32
PS = 256
SIDE = 8
XS = 4
GROUPS = 8
STAGES = 4
HALF = E // 2
PIECE = 4

time_step = 0.25
viscous = 0.5
highest = lax.Precision.HIGHEST
f32 = jnp.float32
bf16 = jnp.bfloat16
i32 = jnp.int32

FAR_FIRST = (4, 3, 5, 2, 6, 1, 7)
OFFSETS = (-2, 2, -1, 1)


def ring(d, size):
    return min(d, size - d)


def split(x):
    hi = x.astype(bf16)
    return hi, (x - hi.astype(f32)).astype(bf16)


def lane_block(rows):
    return lax.broadcasted_iota(i32, (rows, 128), 1) // R


def kernel(
    near_src,
    near_dst,
    near_count,
    far_src,
    far_dst,
    u_hbm,
    s_hbm,
    a_hbm,
    b_hbm,
    blocks_hbm,
    coupling_hbm,
    bases_hbm,
    transfer_hbm,
    coarse_hbm,
    out,
    u_in,
    s_in,
    a_ref,
    b_ref,
    blocks,
    coupling,
    bases,
    transfer,
    coarse,
    near_at,
    near_to,
    far_at,
    w_coefs,
    w_far,
    w_coarse,
    w_bases,
    u_now,
    s_now,
    inverse,
    known,
    tab_a,
    tab_o,
    tab_r,
    tab_b,
    tab_n,
    work_n,
    work_b,
    load_sem,
    a_send,
    a_recv,
    o_send,
    o_recv,
    r_send,
    r_recv,
    b_send,
    b_recv,
    n_send,
    n_recv,
):
    st = lax.axis_index("strike")
    dv = lax.axis_index("dev")
    core = lax.rem(st, 2)
    x = lax.div(st, 2)
    z = lax.div(dv, SIDE)
    y = lax.rem(dv, SIDE)
    other = st + 1 - 2 * core
    my_a = y + core * (z - y)
    my_b = z + core * (y - z)
    step_a = 1 + (SIDE - 1) * core
    step_b = SIDE - (SIDE - 1) * core

    def on_a(d):
        return (st, lax.rem(my_a + d, SIDE) * step_a + my_b * step_b)

    def on_b(d):
        return (st, my_a * step_a + lax.rem(my_b + d, SIDE) * step_b)

    def on_other(d):
        return (other, my_a * step_a + lax.rem(my_b + d, SIDE) * step_b)

    def from_other(d):
        return (other, lax.rem(my_a + d, SIDE) * step_a + my_b * step_b)

    def on_xb(dx, d):
        return (lax.rem(x + dx, XS) * 2 + core, my_a * step_a + lax.rem(my_b + d, SIDE) * step_b)

    far_xb = sorted(
        ((dx, d) for dx in range(XS) for d in range(SIDE) if dx or d),
        key=lambda p: -(ring(p[0], XS) + ring(p[1], SIDE)),
    )

    def has(o):
        return (dv + o >= 0) & (dv + o < SIDE * SIDE)

    loads = [
        (u_hbm.at[:, 0], u_in.at[0]),
        (u_hbm.at[:, 1], u_in.at[1]),
        (bases_hbm, bases),
        (transfer_hbm, transfer),
        (s_hbm.at[:, 0], s_in.at[0]),
        (s_hbm.at[:, 1], s_in.at[1]),
        (a_hbm, a_ref),
        (b_hbm, b_ref),
        (coupling_hbm.at[0], coupling),
        (coarse_hbm, coarse),
        (blocks_hbm.at[0], blocks),
    ]
    loads = [pltpu.make_async_copy(src, dst, load_sem.at[i]) for i, (src, dst) in enumerate(loads)]
    for load in loads:
        load.start()

    tab_n[...] = jnp.zeros_like(tab_n)

    barrier = pltpu.get_barrier_semaphore()
    for dx, d in far_xb:
        pl.semaphore_signal(barrier, inc=1, device_id=on_xb(dx, d))
    for d in FAR_FIRST:
        pl.semaphore_signal(barrier, inc=1, device_id=on_a(d))
    for d in FAR_FIRST + (0,):
        pl.semaphore_signal(barrier, inc=1, device_id=from_other(d))
    n_near = jnp.int32(0)
    for o in OFFSETS:
        n_near = n_near + has(o).astype(i32)

        @pl.when(has(o))
        def _():
            pl.semaphore_signal(barrier, inc=1, device_id=(st, dv + o))

    count = near_count[0]
    for k in range(NB):
        src = near_src[0, k]
        at = (lax.div(src, CL) - dv + REACH) * CL + lax.rem(src, CL)
        near_at[k] = jnp.minimum(jnp.maximum(at, 0), (2 * REACH + 1) * CL - 1)
        for c in range(CL):
            near_to[c, k] = jnp.where((near_dst[0, k] == c) & (count > k), 1.0, 0.0).astype(f32)
    for k in range(NF):
        owner = lax.div(far_src[0, k], CL)
        turned = lax.rem(owner, SIDE) * SIDE + lax.div(owner, SIDE)
        far_at[k] = owner + core * (turned - owner)

    for load in loads[:4]:
        load.wait()

    for c in range(CL):
        row = lax.broadcasted_iota(i32, (R, 128), 0)
        lane = lax.broadcasted_iota(i32, (R, 128), 1)
        placed = ((lane % R == row) & ((lane // R) % CL == c)).astype(f32)
        right = jnp.concatenate([placed] + [transfer[c]] * 4, axis=1)
        w_coefs[c * PS : (c + 1) * PS] = lax.dot_general(
            bases[c].astype(f32), right, (((0,), (0,)), ((), ())), precision=highest, preferred_element_type=f32
        ).astype(bf16)

    for c in range(CL):
        u_now[c] = u_in[c]
    out[...] = jnp.zeros_like(out)

    def prepare():
        for load in loads[4:]:
            load.wait()
        for c in range(CL):
            s_now[c] = s_in[c]
            hi, lo = split(
                jnp.dot(
                    coarse[c].reshape(GROUPS * R, R), bases[c].astype(f32), precision=highest, preferred_element_type=f32
                )
            )
            w_coarse[0 : GROUPS * R, c * PS : (c + 1) * PS] = hi
            w_coarse[GROUPS * R :, c * PS : (c + 1) * PS] = lo
        w_bases[...] = jnp.zeros_like(w_bases)
        for half in range(2):
            for c in range(CL):
                j = half * CL + c
                w_bases[j * R : (j + 1) * R, j * PS : (j + 1) * PS] = bases[c]
        block = lane_block(R)
        for k in range(NF):
            wide = jnp.concatenate([coupling[k]] * 4, axis=1)
            for half in range(2):
                for c in range(CL):
                    lanes = jnp.where(lax.rem(far_src[0, k], CL) == c, half * CL + far_dst[0, k], -1)
                    hi, lo = split(jnp.where(block == lanes, wide, 0.0))
                    at = k * 128 + (half * CL + c) * R
                    w_far[0, at : at + R] = hi
                    w_far[1, at : at + R] = lo

    def near_copy(s, o):
        return pltpu.make_async_remote_copy(
            src_ref=tab_n.at[s, pl.ds(REACH * CL, CL)],
            dst_ref=tab_n.at[s, pl.ds((REACH - o) * CL, CL)],
            send_sem=n_send.at[s, o + REACH],
            recv_sem=n_recv.at[s, REACH - o],
            device_id=(st, dv + o),
        )

    def push(src, dst, send, recv, to):
        pltpu.make_async_remote_copy(
            src_ref=src, dst_ref=dst, send_sem=send, recv_sem=recv, device_id=to
        ).start()

    def wait_blocks(ref, n, sem):
        part = ref.at[pl.ds(0, n)]
        pltpu.make_async_copy(part, part, sem).wait()

    def stage(s, carry):
        for c in range(CL):
            tab_n[s, REACH * CL + c] = (jnp.exp(u_now[c]) - 1.0).astype(bf16)
        deficit = jnp.concatenate([tab_n[s, REACH * CL + c] for c in range(CL)], axis=1)
        both = jnp.dot(deficit, w_coefs[...], preferred_element_type=f32)
        block = lane_block(HALF)
        coefs = jnp.where(block < CL, both[0:HALF, 0:128], both[HALF:E, 0:128])
        share = jnp.where(block == core, both[0:HALF, 128:256], 0.0)
        share = jnp.where(block == CL + core, both[HALF:E, 128:256], share)
        tab_a[s, my_a, 0:HALF] = coefs.astype(bf16)
        tab_a[s, my_a, HALF:E] = share.astype(bf16)
        mine = tab_a.at[s, my_a]
        for d in FAR_FIRST:
            push(mine, mine, a_send.at[s], a_recv.at[s], on_a(d))
            push(mine.at[pl.ds(HALF, HALF)], tab_o.at[s, my_b], o_send.at[s], o_recv.at[s], on_other(d))
        push(mine.at[pl.ds(HALF, HALF)], tab_o.at[s, my_b], o_send.at[s], o_recv.at[s], on_other(0))
        for o in OFFSETS:

            @pl.when(has(o))
            def _():
                near_copy(s, o).start()

        pl.when(s == 0)(prepare)

        wait_blocks(tab_a.at[s], SIDE - 1, a_recv.at[s])
        wait_blocks(tab_o.at[s], SIDE, o_recv.at[s])
        total = jnp.zeros((HALF, 128), f32)
        for i in range(SIDE):
            total = total + tab_a[s, i, HALF:E].astype(f32) + tab_o[s, i].astype(f32)
        tab_r[s, x, my_b] = total.astype(bf16)
        mine = tab_r.at[s, x, my_b]
        for dx, d in far_xb:
            push(mine, mine, r_send.at[s], r_recv.at[s], on_xb(dx, d))
        tab_b[s, my_b] = tab_a[s, :, 0:HALF]
        mine = tab_b.at[s, my_b]
        for d in FAR_FIRST:
            push(mine, mine, b_send.at[s], b_recv.at[s], on_b(d))

        for o in OFFSETS:

            @pl.when(has(-o))
            def _():
                near_copy(s, o).wait_recv()

        work_n[...] = tab_n[s]
        near = jnp.zeros((CL * E, PS), f32)
        for k0 in range(0, NB, PIECE):
            lhs = []
            for k in range(k0, k0 + PIECE):
                rows = work_n[near_at[k]]
                lhs.append(
                    jnp.concatenate(
                        [rows * jnp.full((E, PS), near_to[c, k], f32).astype(bf16) for c in range(CL)],
                        axis=0,
                    )
                )
            near = near + jnp.dot(
                jnp.concatenate(lhs, axis=1),
                blocks[k0 : k0 + PIECE].reshape(PIECE * PS, PS),
                preferred_element_type=f32,
            )

        ahead = jnp.where(s == 2, time_step, 0.5 * time_step).astype(f32)
        weight = jnp.where((s == 1) | (s == 2), 2.0, 1.0).astype(f32)
        for c in range(CL):
            velocity = jnp.exp(u_now[c])
            ds = jnp.exp(-s_now[c]) - velocity
            out[1, c] += weight * ds
            s_now[c] = s_in[c] + ahead * ds
            inverse[c] = 1.0 / (a_ref[c : c + 1] + viscous * velocity)
            known[c] = near[c * E : (c + 1) * E] + b_ref[c : c + 1] * ds

        wait_blocks(tab_b.at[s], SIDE - 1, b_recv.at[s])
        work_b[...] = tab_b[s].reshape(SIDE * SIDE, HALF, 128)
        sources = jnp.concatenate([work_b[far_at[k]] for k in range(NF)], axis=1)
        expansion = jnp.dot(sources, w_far[0], preferred_element_type=f32) + jnp.dot(
            sources, w_far[1], preferred_element_type=f32
        )
        far = jnp.dot(expansion.astype(bf16), w_bases[...], preferred_element_type=f32)
        for c in range(CL):
            for half in range(2):
                j = half * CL + c
                known[c, half * HALF : (half + 1) * HALF] += far[:, j * PS : (j + 1) * PS]

        wait_blocks(tab_r.at[s].reshape(XS * SIDE, HALF, 128), XS * SIDE - 1, r_recv.at[s])
        low = block < CL
        sums = [jnp.sum(tab_r[s, i].astype(f32), axis=0) for i in range(XS)]
        turned = [pltpu.roll(v, 64, 1) for v in sums]
        rows = []
        for half in range(2):
            first, second = (sums, turned) if half == 0 else (turned, sums)
            rows.append(
                jnp.concatenate(
                    [jnp.where(low, first[2 * t], second[2 * t + 1]) for t in range(XS // 2)], axis=1
                )
            )
        groups = jnp.concatenate(rows, axis=0).astype(bf16)
        coarse_far = jnp.dot(
            jnp.concatenate([groups, groups], axis=1), w_coarse[...], preferred_element_type=f32
        )
        for c in range(CL):
            du = -(known[c] + coarse_far[:, c * PS : (c + 1) * PS]) * inverse[c]
            u_now[c] = u_in[c] + ahead * du
            out[0, c] += weight * du

        wait_blocks(tab_a.at[s], SIDE - 1, a_send.at[s])
        wait_blocks(tab_o.at[s], SIDE, o_send.at[s])
        wait_blocks(tab_r.at[s].reshape(XS * SIDE, HALF, 128), XS * SIDE - 1, r_send.at[s])
        wait_blocks(tab_b.at[s], SIDE - 1, b_send.at[s])
        for o in OFFSETS:

            @pl.when(has(o))
            def _():
                near_copy(s, o).wait_send()

        return carry

    pl.semaphore_wait(barrier, XS * SIDE - 1 + 2 * SIDE - 1 + n_near)
    lax.fori_loop(0, STAGES, stage, 0)


def per_device(
    log_rate,
    state_log,
    a_coef,
    b_coef,
    near_src,
    near_dst,
    near_count,
    near_blocks,
    far_src,
    far_dst,
    far_coupling,
    cluster_bases,
    transfer,
    coarse_coupling,
):
    vmem = pl.BlockSpec(memory_space=pltpu.VMEM)
    smem = pl.BlockSpec(memory_space=pltpu.SMEM)
    hbm = pl.BlockSpec(memory_space=pl.ANY)
    state = (CL, E, PS)
    dma = pltpu.SemaphoreType.DMA
    sums = pl.pallas_call(
        kernel,
        out_shape=jax.ShapeDtypeStruct((2, *state), f32),
        in_specs=[smem] * 5 + [hbm] * 9,
        out_specs=vmem,
        scratch_shapes=[
            pltpu.VMEM(state, f32),
            pltpu.VMEM(state, f32),
            pltpu.VMEM((CL, PS), f32),
            pltpu.VMEM((CL, PS), f32),
            pltpu.VMEM((NB, PS, PS), bf16),
            pltpu.VMEM((NF, R, R), f32),
            pltpu.VMEM((CL, R, PS), bf16),
            pltpu.VMEM((CL, R, R), f32),
            pltpu.VMEM((CL, GROUPS, R, R), f32),
            pltpu.SMEM((NB,), i32),
            pltpu.SMEM((CL, NB), f32),
            pltpu.SMEM((NF,), i32),
            pltpu.VMEM((CL * PS, 256), bf16),
            pltpu.VMEM((2, NF * 128, 128), bf16),
            pltpu.VMEM((2 * GROUPS * R, CL * PS), bf16),
            pltpu.VMEM((2 * CL * R, 2 * CL * PS), bf16),
            pltpu.VMEM(state, f32),
            pltpu.VMEM(state, f32),
            pltpu.VMEM(state, f32),
            pltpu.VMEM(state, f32),
            pltpu.VMEM((STAGES, SIDE, E, 128), bf16),
            pltpu.VMEM((STAGES, SIDE, HALF, 128), bf16),
            pltpu.VMEM((STAGES, XS, SIDE, HALF, 128), bf16),
            pltpu.VMEM((STAGES, SIDE, SIDE, HALF, 128), bf16),
            pltpu.VMEM((STAGES, (2 * REACH + 1) * CL, E, PS), bf16),
            pltpu.VMEM(((2 * REACH + 1) * CL, E, PS), bf16),
            pltpu.VMEM((SIDE * SIDE, HALF, 128), bf16),
            dma((11,)),
        ]
        + [dma((STAGES,))] * 8
        + [dma((STAGES, 2 * REACH + 1))] * 2,
        compiler_params=pltpu.CompilerParams(
            collective_id=0, has_side_effects=True, vmem_limit_bytes=56 * 1024 * 1024
        ),
    )(
        near_src,
        near_dst,
        near_count,
        far_src,
        far_dst,
        log_rate,
        state_log,
        a_coef,
        b_coef,
        near_blocks,
        far_coupling,
        cluster_bases,
        transfer,
        coarse_coupling,
    )
    sums = (time_step / 6.0) * sums.transpose(0, 2, 1, 3)
    return log_rate + sums[0], state_log + sums[1]


def solution(mesh):
    cluster = ("strike", "dev")
    state = P(None, cluster, None)
    placed = (
        state,
        state,
        P(cluster, None),
        P(cluster, None),
        P(cluster, None),
        P(cluster, None),
        P(cluster),
        P(cluster, None, None, None),
        P(cluster, None),
        P(cluster, None),
        P(cluster, None, None, None),
        P(cluster, None, None),
        P(cluster, None, None),
        P(cluster, None, None, None),
    )
    return jax.shard_map(
        per_device, mesh=mesh, in_specs=placed, out_specs=(state, state), check_vma=False
    )
```

```python
import jax
import jax.numpy as jnp
from jax import lax
from jax.experimental import pallas as pl
from jax.experimental.pallas import tpu as pltpu
from jax.sharding import PartitionSpec as P

CL = 2
NB = 32
NF = 32
REACH = 2
E = 32
R = 32
PS = 256
SIDE = 8
XS = 4
GROUPS = 8
STAGES = 4
HALF = E // 2
PIECE = 4

time_step = 0.25
viscous = 0.5
highest = lax.Precision.HIGHEST
f32 = jnp.float32
bf16 = jnp.bfloat16
i32 = jnp.int32

FAR_FIRST = (4, 3, 5, 2, 6, 1, 7)
X_FIRST = (2, 1, 3)
OFFSETS = (-2, 2, -1, 1)


def split(x):
    hi = x.astype(bf16)
    return hi, (x - hi.astype(f32)).astype(bf16)


def lane_block(rows):
    return lax.broadcasted_iota(i32, (rows, 128), 1) // R


def kernel(
    near_src_hbm,
    near_dst_hbm,
    near_count_hbm,
    far_src_hbm,
    far_dst_hbm,
    u_hbm,
    s_hbm,
    a_hbm,
    b_hbm,
    blocks_hbm,
    coupling_hbm,
    bases_hbm,
    transfer_hbm,
    coarse_hbm,
    out,
    near_src,
    near_dst,
    near_count,
    far_src,
    far_dst,
    u_in,
    s_in,
    a_ref,
    b_ref,
    blocks,
    coupling,
    bases,
    transfer,
    coarse,
    near_at,
    near_to,
    far_at,
    w_coefs,
    w_far,
    w_coarse,
    w_bases,
    u_now,
    s_now,
    inverse,
    known,
    u_sum,
    s_sum,
    tab_a,
    tab_o,
    tab_p,
    tab_x,
    tab_b,
    tab_n,
    work_n,
    work_b,
    load_sem,
    a_send,
    a_recv,
    o_send,
    o_recv,
    p_send,
    p_recv,
    x_send,
    x_recv,
    b_send,
    b_recv,
    n_send,
    n_recv,
):
    st = lax.axis_index("strike")
    dv = lax.axis_index("dev")
    core = lax.rem(st, 2)
    x = lax.div(st, 2)
    z = lax.div(dv, SIDE)
    y = lax.rem(dv, SIDE)
    other = st + 1 - 2 * core
    my_a = y + core * (z - y)
    my_b = z + core * (y - z)
    step_a = 1 + (SIDE - 1) * core
    step_b = SIDE - (SIDE - 1) * core

    def on_a(d):
        return (st, lax.rem(my_a + d, SIDE) * step_a + my_b * step_b)

    def on_b(d):
        return (st, my_a * step_a + lax.rem(my_b + d, SIDE) * step_b)

    def on_other(d):
        return (other, my_a * step_a + lax.rem(my_b + d, SIDE) * step_b)

    def from_other(d):
        return (other, lax.rem(my_a + d, SIDE) * step_a + my_b * step_b)

    def on_x(d):
        return (lax.rem(x + d, XS) * 2 + core, dv)

    def has(o):
        return (dv + o >= 0) & (dv + o < SIDE * SIDE)

    partners = [to(d) for d in FAR_FIRST for to in (on_a, from_other, on_b)] + [from_other(0)]
    partners += [on_x(d) for d in X_FIRST]
    barrier = pltpu.get_barrier_semaphore()
    for to in partners:
        pl.semaphore_signal(barrier, inc=1, device_id=to)
    n_near = jnp.int32(0)
    for o in OFFSETS:
        n_near = n_near + has(o).astype(i32)

        @pl.when(has(o))
        def _():
            pl.semaphore_signal(barrier, inc=1, device_id=(st, dv + o))

    loads = [
        (u_hbm.at[:, 0], u_in.at[0]),
        (u_hbm.at[:, 1], u_in.at[1]),
        (bases_hbm, bases),
        (transfer_hbm, transfer),
        (near_src_hbm, near_src),
        (near_dst_hbm, near_dst),
        (near_count_hbm, near_count),
        (far_src_hbm, far_src),
        (far_dst_hbm, far_dst),
        (s_hbm.at[:, 0], s_in.at[0]),
        (s_hbm.at[:, 1], s_in.at[1]),
        (a_hbm, a_ref),
        (b_hbm, b_ref),
        (coupling_hbm.at[0], coupling),
        (coarse_hbm, coarse),
        (blocks_hbm.at[0], blocks),
    ]
    loads = [pltpu.make_async_copy(src, dst, load_sem.at[i]) for i, (src, dst) in enumerate(loads)]
    for load in loads:
        load.start()

    for o in OFFSETS:

        @pl.when(jnp.logical_not(has(o)))
        def _():
            empty = jnp.zeros((STAGES, CL, E, PS), bf16)
            tab_n[:, (o + REACH) * CL : (o + REACH + 1) * CL] = empty

    for load in loads[:4]:
        load.wait()

    for c in range(CL):
        row = lax.broadcasted_iota(i32, (R, 128), 0)
        lane = lax.broadcasted_iota(i32, (R, 128), 1)
        placed = ((lane % R == row) & ((lane // R) % CL == c)).astype(f32)
        right = jnp.concatenate([placed] + [transfer[c]] * 4, axis=1)
        w_coefs[c * PS : (c + 1) * PS] = lax.dot_general(
            bases[c].astype(f32), right, (((0,), (0,)), ((), ())), precision=highest, preferred_element_type=f32
        ).astype(bf16)

    for c in range(CL):
        u_now[c] = u_in[c]
    u_sum[...] = jnp.zeros_like(u_sum)
    s_sum[...] = jnp.zeros_like(s_sum)

    def prepare():
        for load in loads[4:]:
            load.wait()
        count = near_count[0]
        for k in range(NB):
            src = near_src[0, k]
            at = (lax.div(src, CL) - dv + REACH) * CL + lax.rem(src, CL)
            near_at[k] = jnp.minimum(jnp.maximum(at, 0), (2 * REACH + 1) * CL - 1)
            for c in range(CL):
                near_to[c, k] = jnp.where((near_dst[0, k] == c) & (count > k), 1.0, 0.0).astype(f32)
        for k in range(NF):
            owner = lax.div(far_src[0, k], CL)
            turned = lax.rem(owner, SIDE) * SIDE + lax.div(owner, SIDE)
            far_at[k] = owner + core * (turned - owner)
        for c in range(CL):
            s_now[c] = s_in[c]
            hi, lo = split(
                jnp.dot(
                    coarse[c].reshape(GROUPS * R, R), bases[c].astype(f32), precision=highest, preferred_element_type=f32
                )
            )
            w_coarse[0 : GROUPS * R, c * PS : (c + 1) * PS] = hi
            w_coarse[GROUPS * R :, c * PS : (c + 1) * PS] = lo
        w_bases[...] = jnp.zeros_like(w_bases)
        for half in range(2):
            for c in range(CL):
                j = half * CL + c
                w_bases[j * R : (j + 1) * R, j * PS : (j + 1) * PS] = bases[c]
        wide_block = lane_block(R)
        for k in range(NF):
            wide = jnp.concatenate([coupling[k]] * 4, axis=1)
            for half in range(2):
                for c in range(CL):
                    lanes = jnp.where(lax.rem(far_src[0, k], CL) == c, half * CL + far_dst[0, k], -1)
                    hi, lo = split(jnp.where(wide_block == lanes, wide, 0.0))
                    at = k * 128 + (half * CL + c) * R
                    w_far[0, at : at + R] = hi
                    w_far[1, at : at + R] = lo

    def near_copy(s, o):
        return pltpu.make_async_remote_copy(
            src_ref=tab_n.at[s, pl.ds(REACH * CL, CL)],
            dst_ref=tab_n.at[s, pl.ds((REACH - o) * CL, CL)],
            send_sem=n_send.at[s, o + REACH],
            recv_sem=n_recv.at[s, REACH - o],
            device_id=(st, dv + o),
        )

    def push(src, dst, send, recv, to):
        pltpu.make_async_remote_copy(
            src_ref=src, dst_ref=dst, send_sem=send, recv_sem=recv, device_id=to
        ).start()

    def wait_blocks(ref, n, sem):
        part = ref.at[pl.ds(0, n)]
        pltpu.make_async_copy(part, part, sem).wait()

    block = lane_block(HALF)

    def begin(s):
        for c in range(CL):
            tab_n[s, REACH * CL + c] = (jnp.exp(u_now[c]) - 1.0).astype(bf16)
        deficit = jnp.concatenate([tab_n[s, REACH * CL + c] for c in range(CL)], axis=1)
        both = jnp.dot(deficit, w_coefs[...], preferred_element_type=f32)
        coefs = jnp.where(block < CL, both[0:HALF, 0:128], both[HALF:E, 0:128])
        share = jnp.where(block == core, both[0:HALF, 128:256], 0.0)
        share = jnp.where(block == CL + core, both[HALF:E, 128:256], share)
        tab_a[s, my_a, 0:HALF] = coefs.astype(bf16)
        tab_a[s, my_a, HALF:E] = share.astype(bf16)

    def wait_sends(s):
        wait_blocks(tab_a.at[s], SIDE - 1, a_send.at[s])
        wait_blocks(tab_o.at[s], SIDE, o_send.at[s])
        wait_blocks(tab_p.at[s], SIDE - 1, p_send.at[s])
        wait_blocks(tab_x.at[s], XS - 1, x_send.at[s])
        wait_blocks(tab_b.at[s], SIDE - 1, b_send.at[s])
        for o in OFFSETS:

            @pl.when(has(o))
            def _():
                near_copy(s, o).wait_send()

    def stage(s, carry):
        mine = tab_a.at[s, my_a]
        share = mine.at[pl.ds(HALF, HALF)]
        for d in FAR_FIRST:
            push(mine, mine, a_send.at[s], a_recv.at[s], on_a(d))
            push(share, tab_o.at[s, my_b], o_send.at[s], o_recv.at[s], on_other(d))
        push(share, tab_o.at[s, my_b], o_send.at[s], o_recv.at[s], on_other(0))
        for o in OFFSETS:

            @pl.when(has(o))
            def _():
                near_copy(s, o).start()

        pl.when(s == 0)(prepare)
        pl.when(s > 0)(lambda: wait_sends(s - 1))

        wait_blocks(tab_a.at[s], SIDE - 1, a_recv.at[s])
        wait_blocks(tab_o.at[s], SIDE, o_recv.at[s])
        row_sum = jnp.sum(tab_a[s, :, HALF:E].astype(f32) + tab_o[s].astype(f32), axis=0)
        tab_p[s, my_b] = row_sum.astype(bf16)
        mine = tab_p.at[s, my_b]
        for d in FAR_FIRST:
            push(mine, mine, p_send.at[s], p_recv.at[s], on_b(d))
        tab_b[s, my_b] = tab_a[s, :, 0:HALF]
        mine = tab_b.at[s, my_b]
        for d in FAR_FIRST:
            push(mine, mine, b_send.at[s], b_recv.at[s], on_b(d))

        wait_blocks(tab_p.at[s], SIDE - 1, p_recv.at[s])
        tab_x[s, x] = jnp.sum(tab_p[s].astype(f32), axis=0).astype(bf16)
        mine = tab_x.at[s, x]
        for d in X_FIRST:
            push(mine, mine, x_send.at[s], x_recv.at[s], on_x(d))

        for o in OFFSETS:

            @pl.when(has(-o))
            def _():
                near_copy(s, o).wait_recv()

        work_n[...] = tab_n[s]
        near = jnp.zeros((CL * E, PS), f32)
        for k0 in range(0, NB, PIECE):
            lhs = []
            for k in range(k0, k0 + PIECE):
                rows = work_n[near_at[k]]
                lhs.append(
                    jnp.concatenate(
                        [rows * jnp.full((E, PS), near_to[c, k], f32).astype(bf16) for c in range(CL)],
                        axis=0,
                    )
                )
            near = near + jnp.dot(
                jnp.concatenate(lhs, axis=1),
                blocks[k0 : k0 + PIECE].reshape(PIECE * PS, PS),
                preferred_element_type=f32,
            )

        ahead = jnp.where(s == 2, time_step, 0.5 * time_step).astype(f32)
        weight = jnp.where((s == 1) | (s == 2), 2.0, 1.0).astype(f32)
        for c in range(CL):
            velocity = jnp.exp(u_now[c])
            ds = jnp.exp(-s_now[c]) - velocity
            s_sum[c] += weight * ds
            s_now[c] = s_in[c] + ahead * ds
            inverse[c] = 1.0 / (a_ref[c : c + 1] + viscous * velocity)
            known[c] = near[c * E : (c + 1) * E] + b_ref[c : c + 1] * ds

        wait_blocks(tab_b.at[s], SIDE - 1, b_recv.at[s])
        work_b[...] = tab_b[s].reshape(SIDE * SIDE, HALF, 128)
        sources = jnp.concatenate([work_b[far_at[k]] for k in range(NF)], axis=1)
        expansion = jnp.dot(sources, w_far[0], preferred_element_type=f32) + jnp.dot(
            sources, w_far[1], preferred_element_type=f32
        )
        far = jnp.dot(expansion.astype(bf16), w_bases[...], preferred_element_type=f32)
        for c in range(CL):
            for half in range(2):
                j = half * CL + c
                known[c, half * HALF : (half + 1) * HALF] += far[:, j * PS : (j + 1) * PS]

        wait_blocks(tab_x.at[s], XS - 1, x_recv.at[s])
        low = block < CL
        sums = [tab_x[s, i].astype(f32) for i in range(XS)]
        turned = [pltpu.roll(v, 64, 1) for v in sums]
        rows = []
        for half in range(2):
            first, second = (sums, turned) if half == 0 else (turned, sums)
            rows.append(
                jnp.concatenate(
                    [jnp.where(low, first[2 * t], second[2 * t + 1]) for t in range(XS // 2)], axis=1
                )
            )
        groups = jnp.concatenate(rows, axis=0).astype(bf16)
        coarse_far = jnp.dot(
            jnp.concatenate([groups, groups], axis=1), w_coarse[...], preferred_element_type=f32
        )
        for c in range(CL):
            du = -(known[c] + coarse_far[:, c * PS : (c + 1) * PS]) * inverse[c]
            u_now[c] = u_in[c] + ahead * du
            u_sum[c] += weight * du

        pl.when(s < STAGES - 1)(lambda: begin(s + 1))
        return carry

    begin(0)
    pl.semaphore_wait(barrier, len(partners) + n_near)
    lax.fori_loop(0, STAGES, stage, 0)
    wait_sends(STAGES - 1)
    for c in range(CL):
        out[0, :, c] = (time_step / 6.0) * u_sum[c]
        out[1, :, c] = (time_step / 6.0) * s_sum[c]


def per_device(
    log_rate,
    state_log,
    a_coef,
    b_coef,
    near_src,
    near_dst,
    near_count,
    near_blocks,
    far_src,
    far_dst,
    far_coupling,
    cluster_bases,
    transfer,
    coarse_coupling,
):
    vmem = pl.BlockSpec(memory_space=pltpu.VMEM)
    hbm = pl.BlockSpec(memory_space=pl.ANY)
    state = (CL, E, PS)
    dma = pltpu.SemaphoreType.DMA
    step = pl.pallas_call(
        kernel,
        out_shape=jax.ShapeDtypeStruct((2, E, CL, PS), f32),
        in_specs=[hbm] * 14,
        out_specs=vmem,
        scratch_shapes=[
            pltpu.SMEM((1, NB), i32),
            pltpu.SMEM((1, NB), i32),
            pltpu.SMEM((1,), i32),
            pltpu.SMEM((1, NF), i32),
            pltpu.SMEM((1, NF), i32),
            pltpu.VMEM(state, f32),
            pltpu.VMEM(state, f32),
            pltpu.VMEM((CL, PS), f32),
            pltpu.VMEM((CL, PS), f32),
            pltpu.VMEM((NB, PS, PS), bf16),
            pltpu.VMEM((NF, R, R), f32),
            pltpu.VMEM((CL, R, PS), bf16),
            pltpu.VMEM((CL, R, R), f32),
            pltpu.VMEM((CL, GROUPS, R, R), f32),
            pltpu.SMEM((NB,), i32),
            pltpu.SMEM((CL, NB), f32),
            pltpu.SMEM((NF,), i32),
            pltpu.VMEM((CL * PS, 256), bf16),
            pltpu.VMEM((2, NF * 128, 128), bf16),
            pltpu.VMEM((2 * GROUPS * R, CL * PS), bf16),
            pltpu.VMEM((2 * CL * R, 2 * CL * PS), bf16),
            pltpu.VMEM(state, f32),
            pltpu.VMEM(state, f32),
            pltpu.VMEM(state, f32),
            pltpu.VMEM(state, f32),
            pltpu.VMEM(state, f32),
            pltpu.VMEM(state, f32),
            pltpu.VMEM((STAGES, SIDE, E, 128), bf16),
            pltpu.VMEM((STAGES, SIDE, HALF, 128), bf16),
            pltpu.VMEM((STAGES, SIDE, HALF, 128), bf16),
            pltpu.VMEM((STAGES, XS, HALF, 128), bf16),
            pltpu.VMEM((STAGES, SIDE, SIDE, HALF, 128), bf16),
            pltpu.VMEM((STAGES, (2 * REACH + 1) * CL, E, PS), bf16),
            pltpu.VMEM(((2 * REACH + 1) * CL, E, PS), bf16),
            pltpu.VMEM((SIDE * SIDE, HALF, 128), bf16),
            dma((16,)),
        ]
        + [dma((STAGES,))] * 10
        + [dma((STAGES, 2 * REACH + 1))] * 2,
        compiler_params=pltpu.CompilerParams(
            collective_id=0, has_side_effects=True, vmem_limit_bytes=56 * 1024 * 1024
        ),
    )(
        near_src,
        near_dst,
        near_count,
        far_src,
        far_dst,
        log_rate,
        state_log,
        a_coef,
        b_coef,
        near_blocks,
        far_coupling,
        cluster_bases,
        transfer,
        coarse_coupling,
    )
    return log_rate + step[0], state_log + step[1]


def solution(mesh):
    cluster = ("strike", "dev")
    state = P(None, cluster, None)
    placed = (
        state,
        state,
        P(cluster, None),
        P(cluster, None),
        P(cluster, None),
        P(cluster, None),
        P(cluster),
        P(cluster, None, None, None),
        P(cluster, None),
        P(cluster, None),
        P(cluster, None, None, None),
        P(cluster, None, None),
        P(cluster, None, None),
        P(cluster, None, None, None),
    )
    return jax.shard_map(
        per_device, mesh=mesh, in_specs=placed, out_specs=(state, state), check_vma=False
    )
```

```python
import jax
import jax.numpy as jnp
from jax import lax
from jax.experimental import pallas as pl
from jax.experimental.pallas import tpu as pltpu
from jax.sharding import PartitionSpec as P

CL = 2
NB = 32
NF = 32
REACH = 2
E = 32
R = 32
PS = 256
SIDE = 8
XS = 4
GROUPS = 8
STAGES = 4
HALF = E // 2
PIECE = 4

time_step = 0.25
viscous = 0.5
highest = lax.Precision.HIGHEST
f32 = jnp.float32
bf16 = jnp.bfloat16
i32 = jnp.int32

FAR_FIRST = (4, 3, 5, 2, 6, 1, 7)
FIRST = 12
OFFSETS = (-2, 2, -1, 1)


def ring(d, size):
    return min(d, size - d)


def split(x):
    hi = x.astype(bf16)
    return hi, (x - hi.astype(f32)).astype(bf16)


def lane_block(rows):
    return lax.broadcasted_iota(i32, (rows, 128), 1) // R


def kernel(
    near_src_hbm,
    near_dst_hbm,
    near_count_hbm,
    far_src_hbm,
    far_dst_hbm,
    u_hbm,
    s_hbm,
    a_hbm,
    b_hbm,
    blocks_hbm,
    coupling_hbm,
    bases_hbm,
    transfer_hbm,
    coarse_hbm,
    out,
    near_src,
    near_dst,
    near_count,
    u_in,
    s_in,
    a_ref,
    b_ref,
    blocks,
    far_src_row,
    far_dst_row,
    coupling,
    bases,
    transfer,
    coarse,
    near_at,
    near_to,
    w_coefs,
    w_built,
    w_sent,
    w_came,
    w_own,
    w_far,
    w_sum,
    u_now,
    s_now,
    inverse,
    known,
    u_sum,
    s_sum,
    tab_a,
    tab_o,
    tab_r,
    tab_b,
    tab_f,
    part_f,
    expansion,
    tab_n,
    work_n,
    load_sem,
    coupling_sem,
    a_send,
    a_recv,
    o_send,
    o_recv,
    r_send,
    r_recv,
    f_send,
    f_recv,
    b_send,
    b_recv,
    w_send,
    w_recv,
    n_send,
    n_recv,
):
    st = lax.axis_index("strike")
    dv = lax.axis_index("dev")
    core = lax.rem(st, 2)
    x = lax.div(st, 2)
    z = lax.div(dv, SIDE)
    y = lax.rem(dv, SIDE)
    other = st + 1 - 2 * core
    my_a = y + core * (z - y)
    my_b = z + core * (y - z)
    step_a = 1 + (SIDE - 1) * core
    step_b = SIDE - (SIDE - 1) * core

    def on_a(d):
        return (st, lax.rem(my_a + d, SIDE) * step_a + my_b * step_b)

    def on_b(d):
        return (st, my_a * step_a + lax.rem(my_b + d, SIDE) * step_b)

    def on_other(d):
        return (other, my_a * step_a + lax.rem(my_b + d, SIDE) * step_b)

    def from_other(d):
        return (other, lax.rem(my_a + d, SIDE) * step_a + my_b * step_b)

    def on_xb(dx, d):
        return (lax.rem(x + dx, XS) * 2 + core, my_a * step_a + lax.rem(my_b + d, SIDE) * step_b)

    far_xb = sorted(
        ((dx, d) for dx in range(XS) for d in range(SIDE) if dx or d),
        key=lambda p: -(ring(p[0], XS) + ring(p[1], SIDE)),
    )

    def has(o):
        return (dv + o >= 0) & (dv + o < SIDE * SIDE)

    partners = [on_xb(dx, d) for dx, d in far_xb]
    partners += [to(d) for d in FAR_FIRST for to in (on_a, from_other)] + [from_other(0)]
    barrier = pltpu.get_barrier_semaphore()
    for to in partners:
        pl.semaphore_signal(barrier, inc=1, device_id=to)
    n_near = jnp.int32(0)
    for o in OFFSETS:
        n_near = n_near + has(o).astype(i32)

        @pl.when(has(o))
        def _():
            pl.semaphore_signal(barrier, inc=1, device_id=(st, dv + o))

    loads = [
        (u_hbm.at[:, 0], u_in.at[0]),
        (u_hbm.at[:, 1], u_in.at[1]),
        (bases_hbm, bases),
        (transfer_hbm, transfer),
        (near_src_hbm, near_src),
        (near_dst_hbm, near_dst),
        (near_count_hbm, near_count),
        (far_src_hbm, far_src_row),
        (far_dst_hbm, far_dst_row),
        (s_hbm.at[:, 0], s_in.at[0]),
        (s_hbm.at[:, 1], s_in.at[1]),
        (a_hbm, a_ref),
        (b_hbm, b_ref),
        (coarse_hbm, coarse),
        (blocks_hbm.at[0], blocks),
    ]
    loads = [pltpu.make_async_copy(src, dst, load_sem.at[i]) for i, (src, dst) in enumerate(loads)]
    for load in loads[:4]:
        load.start()
    for r in range(R):
        pltpu.make_async_copy(coupling_hbm.at[0, :, r], coupling.at[r], coupling_sem).start()
    for load in loads[4:]:
        load.start()

    for o in OFFSETS:

        @pl.when(jnp.logical_not(has(o)))
        def _():
            empty = jnp.zeros((STAGES, CL, E, PS), bf16)
            tab_n[:, (o + REACH) * CL : (o + REACH + 1) * CL] = empty

    for load in loads[:4]:
        load.wait()

    for c in range(CL):
        row = lax.broadcasted_iota(i32, (R, 128), 0)
        lane = lax.broadcasted_iota(i32, (R, 128), 1)
        placed = ((lane % R == row) & ((lane // R) % CL == c)).astype(f32)
        right = jnp.concatenate([placed] + [transfer[c]] * 4, axis=1)
        w_coefs[c * PS : (c + 1) * PS] = lax.dot_general(
            bases[c].astype(f32), right, (((0,), (0,)), ((), ())), precision=highest, preferred_element_type=f32
        ).astype(bf16)

    for c in range(CL):
        u_now[c] = u_in[c]
    u_sum[...] = jnp.zeros_like(u_sum)
    s_sum[...] = jnp.zeros_like(s_sum)

    def build_far():
        for load in loads[4:9]:
            load.wait()
        pltpu.make_async_copy(coupling, coupling, coupling_sem).wait()
        src = far_src_row[...]
        owner = src >> 1
        its_y, its_z = owner & (SIDE - 1), owner >> 3
        its_a, its_b = its_y + core * (its_z - its_y), its_z + core * (its_y - its_z)
        place = jnp.concatenate([its_b * SIDE + its_a] * 4, axis=1)
        kind = jnp.concatenate([(src & 1) * CL + far_dst_row[...]] * 4, axis=1)
        places = SIDE * SIDE
        chosen = (lax.broadcasted_iota(i32, (places, 128), 0) == place) & (lane_block(places) == kind)
        chosen = jnp.where(chosen, 1.0, 0.0).astype(bf16)
        chosen = jnp.concatenate([chosen, chosen], axis=1)
        quarter = lane_block(NF)

        def rows_of(r4, carry):
            for i in range(4):
                r = r4 * 4 + i
                wide = jnp.concatenate([coupling[r]] * 4, axis=1)
                parts = [split(jnp.where(quarter == j, wide, 0.0)) for j in range(4)]
                right = jnp.concatenate([p[0] for p in parts] + [p[1] for p in parts], axis=0)
                rows = jnp.dot(chosen, right, preferred_element_type=f32)
                at = pl.ds(pl.multiple_of(r * SIDE, SIDE), SIDE)
                w_built[:, at] = rows.reshape(SIDE, SIDE, 128)
            return carry

        lax.fori_loop(0, R // 4, rows_of, 0)
        for b in range(SIDE):
            for a in range(SIDE):
                w_sent[b, a] = w_built[b, pl.ds(a, R, stride=SIDE), :].astype(bf16)
        w_came[my_b] = w_sent[my_b]

        def unpack_own(b, carry):
            unpack(w_sent, b, lambda a, j: w_own.at[pl.ds(pl.multiple_of(b * SIDE * 128 + a * 128 + j * R, R), R)])
            return carry

        lax.fori_loop(0, SIDE, unpack_own, 0)

    def unpack(packed, b, to):
        low = lax.broadcasted_iota(i32, (R, 128), 1) < 64
        for a in range(SIDE):
            block = packed[b, a].astype(f32)
            turned = pltpu.roll(block, 64, 1)
            for j, (here, mask) in enumerate(((block, low), (turned, low), (turned, ~low), (block, ~low))):
                to(a, j)[...] = jnp.where(mask, here, 0.0).astype(bf16)

    def unpack_far():
        wait_blocks(w_came, SIDE - 1, w_recv)

        def column_of(b, carry):
            at = pl.ds(pl.multiple_of(b * 128, 128), 128)
            unpack(w_came, b, lambda a, j: w_far.at[pl.ds(a * 128 + j * R, R), at])
            return carry

        lax.fori_loop(0, SIDE, column_of, 0)

    def prepare():
        for load in loads[9:]:
            load.wait()
        count = near_count[0]
        for k in range(NB):
            src = near_src[0, k]
            at = (lax.div(src, CL) - dv + REACH) * CL + lax.rem(src, CL)
            near_at[k] = jnp.minimum(jnp.maximum(at, 0), (2 * REACH + 1) * CL - 1)
            for c in range(CL):
                near_to[c, k] = jnp.where((near_dst[0, k] == c) & (count > k), 1.0, 0.0).astype(f32)
        for c in range(CL):
            s_now[c] = s_in[c]
            hi, lo = split(
                jnp.dot(
                    coarse[c].reshape(GROUPS * R, R), bases[c].astype(f32), precision=highest, preferred_element_type=f32
                )
            )
            w_sum[0 : GROUPS * R, c * PS : (c + 1) * PS] = hi
            w_sum[GROUPS * R : 2 * GROUPS * R, c * PS : (c + 1) * PS] = lo
        w_sum[2 * GROUPS * R :] = jnp.zeros((128, CL * PS), bf16)
        for c in range(CL):
            at = 2 * GROUPS * R + c * R
            w_sum[at : at + R, c * PS : (c + 1) * PS] = bases[c]

    def near_copy(s, o):
        return pltpu.make_async_remote_copy(
            src_ref=tab_n.at[s, pl.ds(REACH * CL, CL)],
            dst_ref=tab_n.at[s, pl.ds((REACH - o) * CL, CL)],
            send_sem=n_send.at[s, o + REACH],
            recv_sem=n_recv.at[s, REACH - o],
            device_id=(st, dv + o),
        )

    def push(src, dst, send, recv, to):
        pltpu.make_async_remote_copy(
            src_ref=src, dst_ref=dst, send_sem=send, recv_sem=recv, device_id=to
        ).start()

    def wait_blocks(ref, n, sem):
        part = ref.at[pl.ds(0, n)]
        pltpu.make_async_copy(part, part, sem).wait()

    block = lane_block(HALF)

    def begin(s):
        for c in range(CL):
            tab_n[s, REACH * CL + c] = (jnp.exp(u_now[c]) - 1.0).astype(bf16)
        deficit = jnp.concatenate([tab_n[s, REACH * CL + c] for c in range(CL)], axis=1)
        both = jnp.dot(deficit, w_coefs[...], preferred_element_type=f32)
        coefs = jnp.where(block < CL, both[0:HALF, 0:128], both[HALF:E, 0:128])
        share = jnp.where(block == core, both[0:HALF, 128:256], 0.0)
        share = jnp.where(block == CL + core, both[HALF:E, 128:256], share)
        tab_a[s, my_a, 0:HALF] = coefs.astype(bf16)
        tab_a[s, my_a, HALF:E] = share.astype(bf16)

    def wait_sends(s):
        wait_blocks(tab_a.at[s], SIDE - 1, a_send.at[s])
        wait_blocks(tab_o.at[s], SIDE, o_send.at[s])
        wait_blocks(tab_r.at[s].reshape(XS * SIDE, HALF, 128), XS * SIDE - 1, r_send.at[s])
        for o in OFFSETS:

            @pl.when(has(o))
            def _():
                near_copy(s, o).wait_send()

    def send_first():
        tab_b[my_b] = tab_a[0, :, 0:HALF]
        for d in FAR_FIRST:
            push(tab_b.at[my_b], tab_b.at[my_b], b_send, b_recv, on_b(d))
        for d in FAR_FIRST:
            push(w_sent.at[lax.rem(my_b + d, SIDE)], w_came.at[my_b], w_send, w_recv, on_b(d))

    def far_first():
        wait_blocks(tab_b, SIDE - 1, b_recv)
        sources = jnp.concatenate([tab_b[b, a] for b in range(SIDE) for a in range(SIDE)], axis=1)
        expansion[...] = jnp.dot(sources, w_own[...], preferred_element_type=f32)

    def far_later(s):
        wait_blocks(tab_f.at[s], SIDE - 1, f_recv.at[s])
        expansion[...] = jnp.sum(tab_f[s].astype(f32), axis=0)

    def send_far(s):
        sources = jnp.concatenate([tab_a[s, i, 0:HALF] for i in range(SIDE)], axis=1)
        parts = jnp.dot(sources, w_far[...], preferred_element_type=f32).astype(bf16)
        for i in range(SIDE):
            part_f[s, i] = parts[:, i * 128 : (i + 1) * 128]
        for d in FAR_FIRST:
            push(part_f.at[s, lax.rem(my_b + d, SIDE)], tab_f.at[s, my_b], f_send.at[s], f_recv.at[s], on_b(d))
        tab_f[s, my_b] = part_f[s, my_b]

    def stage(s, carry):
        mine = tab_a.at[s, my_a]
        share = mine.at[pl.ds(HALF, HALF)]
        for d in FAR_FIRST:
            push(mine, mine, a_send.at[s], a_recv.at[s], on_a(d))
            push(share, tab_o.at[s, my_b], o_send.at[s], o_recv.at[s], on_other(d))
        push(share, tab_o.at[s, my_b], o_send.at[s], o_recv.at[s], on_other(0))
        for o in OFFSETS:

            @pl.when(has(o))
            def _():
                near_copy(s, o).start()

        pl.when(s == 0)(build_far)
        pl.when(s == 0)(prepare)
        pl.when(s == 1)(unpack_far)
        pl.when(s > 0)(lambda: wait_sends(s - 1))

        wait_blocks(tab_a.at[s], SIDE - 1, a_recv.at[s])
        wait_blocks(tab_o.at[s], SIDE, o_recv.at[s])
        row_sum = jnp.sum(tab_a[s, :, HALF:E].astype(f32) + tab_o[s].astype(f32), axis=0)
        tab_r[s, x, my_b] = row_sum.astype(bf16)
        mine = tab_r.at[s, x, my_b]
        for dx, d in far_xb[:FIRST]:
            push(mine, mine, r_send.at[s], r_recv.at[s], on_xb(dx, d))
        pl.when(s > 0)(lambda: send_far(s))
        for dx, d in far_xb[FIRST:]:
            push(mine, mine, r_send.at[s], r_recv.at[s], on_xb(dx, d))

        pl.when(s == 0)(send_first)

        for o in OFFSETS:

            @pl.when(has(-o))
            def _():
                near_copy(s, o).wait_recv()

        work_n[...] = tab_n[s]
        near = jnp.zeros((CL * E, PS), f32)
        for k0 in range(0, NB, PIECE):
            lhs = []
            for k in range(k0, k0 + PIECE):
                rows = work_n[near_at[k]]
                lhs.append(
                    jnp.concatenate(
                        [rows * jnp.full((E, PS), near_to[c, k], f32).astype(bf16) for c in range(CL)],
                        axis=0,
                    )
                )
            near = near + jnp.dot(
                jnp.concatenate(lhs, axis=1),
                blocks[k0 : k0 + PIECE].reshape(PIECE * PS, PS),
                preferred_element_type=f32,
            )

        ahead = jnp.where(s == 2, time_step, 0.5 * time_step).astype(f32)
        weight = jnp.where((s == 1) | (s == 2), 2.0, 1.0).astype(f32)
        for c in range(CL):
            velocity = jnp.exp(u_now[c])
            ds = jnp.exp(-s_now[c]) - velocity
            s_sum[c] += weight * ds
            s_now[c] = s_in[c] + ahead * ds
            inverse[c] = 1.0 / (a_ref[c : c + 1] + viscous * velocity)
            known[c] = near[c * E : (c + 1) * E] + b_ref[c : c + 1] * ds

        pl.when(s == 0)(far_first)
        pl.when(s > 0)(lambda: far_later(s))
        halves = jnp.concatenate([expansion[...], pltpu.roll(expansion[...], 64, 1)], axis=0).astype(bf16)
        wait_blocks(tab_r.at[s].reshape(XS * SIDE, HALF, 128), XS * SIDE - 1, r_recv.at[s])
        low = block < CL
        sums = [jnp.sum(tab_r[s, i].astype(f32), axis=0) for i in range(XS)]
        turned = [pltpu.roll(v, 64, 1) for v in sums]
        rows = []
        for half in range(2):
            first, second = (sums, turned) if half == 0 else (turned, sums)
            rows.append(
                jnp.concatenate(
                    [jnp.where(low, first[2 * t], second[2 * t + 1]) for t in range(XS // 2)], axis=1
                )
            )
        groups = jnp.concatenate(rows, axis=0).astype(bf16)
        far = jnp.dot(
            jnp.concatenate([groups, groups, halves], axis=1), w_sum[...], preferred_element_type=f32
        )
        for c in range(CL):
            du = -(known[c] + far[:, c * PS : (c + 1) * PS]) * inverse[c]
            u_now[c] = u_in[c] + ahead * du
            u_sum[c] += weight * du

        pl.when(s < STAGES - 1)(lambda: begin(s + 1))
        return carry

    begin(0)
    pl.semaphore_wait(barrier, len(partners) + n_near)
    lax.fori_loop(0, STAGES, stage, 0)
    wait_sends(STAGES - 1)
    wait_blocks(tab_b, SIDE - 1, b_send)
    wait_blocks(w_came, SIDE - 1, w_send)
    for s in range(1, STAGES):
        wait_blocks(tab_f.at[s], SIDE - 1, f_send.at[s])
    for c in range(CL):
        out[0, :, c] = (time_step / 6.0) * u_sum[c]
        out[1, :, c] = (time_step / 6.0) * s_sum[c]


def per_device(
    log_rate,
    state_log,
    a_coef,
    b_coef,
    near_src,
    near_dst,
    near_count,
    near_blocks,
    far_src,
    far_dst,
    far_coupling,
    cluster_bases,
    transfer,
    coarse_coupling,
):
    vmem = pl.BlockSpec(memory_space=pltpu.VMEM)
    hbm = pl.BlockSpec(memory_space=pl.ANY)
    state = (CL, E, PS)
    dma = pltpu.SemaphoreType.DMA
    step = pl.pallas_call(
        kernel,
        out_shape=jax.ShapeDtypeStruct((2, E, CL, PS), f32),
        in_specs=[hbm] * 14,
        out_specs=vmem,
        scratch_shapes=[
            pltpu.SMEM((1, NB), i32),
            pltpu.SMEM((1, NB), i32),
            pltpu.SMEM((1,), i32),
            pltpu.VMEM(state, f32),
            pltpu.VMEM(state, f32),
            pltpu.VMEM((CL, PS), f32),
            pltpu.VMEM((CL, PS), f32),
            pltpu.VMEM((NB, PS, PS), bf16),
            pltpu.VMEM((1, NF), i32),
            pltpu.VMEM((1, NF), i32),
            pltpu.VMEM((R, NF, R), f32),
            pltpu.VMEM((CL, R, PS), bf16),
            pltpu.VMEM((CL, R, R), f32),
            pltpu.VMEM((CL, GROUPS, R, R), f32),
            pltpu.SMEM((NB,), i32),
            pltpu.SMEM((CL, NB), f32),
            pltpu.VMEM((CL * PS, 256), bf16),
            pltpu.VMEM((SIDE, R * SIDE, 128), f32),
            pltpu.VMEM((SIDE, SIDE, R, 128), bf16),
            pltpu.VMEM((SIDE, SIDE, R, 128), bf16),
            pltpu.VMEM((SIDE * SIDE * 128, 128), bf16),
            pltpu.VMEM((SIDE * 128, SIDE * 128), bf16),
            pltpu.VMEM((2 * GROUPS * R + 128, CL * PS), bf16),
            pltpu.VMEM(state, f32),
            pltpu.VMEM(state, f32),
            pltpu.VMEM(state, f32),
            pltpu.VMEM(state, f32),
            pltpu.VMEM(state, f32),
            pltpu.VMEM(state, f32),
            pltpu.VMEM((STAGES, SIDE, E, 128), bf16),
            pltpu.VMEM((STAGES, SIDE, HALF, 128), bf16),
            pltpu.VMEM((STAGES, XS, SIDE, HALF, 128), bf16),
            pltpu.VMEM((SIDE, SIDE, HALF, 128), bf16),
            pltpu.VMEM((STAGES, SIDE, HALF, 128), bf16),
            pltpu.VMEM((STAGES, SIDE, HALF, 128), bf16),
            pltpu.VMEM((HALF, 128), f32),
            pltpu.VMEM((STAGES, (2 * REACH + 1) * CL, E, PS), bf16),
            pltpu.VMEM(((2 * REACH + 1) * CL, E, PS), bf16),
            dma((15,)),
            dma,
        ]
        + [dma((STAGES,))] * 8
        + [dma] * 4
        + [dma((STAGES, 2 * REACH + 1))] * 2,
        compiler_params=pltpu.CompilerParams(
            collective_id=0, has_side_effects=True, vmem_limit_bytes=56 * 1024 * 1024
        ),
    )(
        near_src,
        near_dst,
        near_count,
        far_src,
        far_dst,
        log_rate,
        state_log,
        a_coef,
        b_coef,
        near_blocks,
        far_coupling,
        cluster_bases,
        transfer,
        coarse_coupling,
    )
    return log_rate + step[0], state_log + step[1]


def solution(mesh):
    cluster = ("strike", "dev")
    state = P(None, cluster, None)
    placed = (
        state,
        state,
        P(cluster, None),
        P(cluster, None),
        P(cluster, None),
        P(cluster, None),
        P(cluster),
        P(cluster, None, None, None),
        P(cluster, None),
        P(cluster, None),
        P(cluster, None, None, None),
        P(cluster, None, None),
        P(cluster, None, None),
        P(cluster, None, None, None),
    )
    return jax.shard_map(
        per_device, mesh=mesh, in_specs=placed, out_specs=(state, state), check_vma=False
    )
```

```python
import jax
import jax.numpy as jnp
from jax import lax
from jax.experimental import pallas as pl
from jax.experimental.pallas import tpu as pltpu
from jax.sharding import PartitionSpec as P

CL = 2
NB = 32
NF = 32
REACH = 2
E = 32
R = 32
PS = 256
SIDE = 8
XS = 4
GROUPS = 8
STAGES = 4
HALF = E // 2
PIECE = 4

time_step = 0.25
viscous = 0.5
highest = lax.Precision.HIGHEST
f32 = jnp.float32
bf16 = jnp.bfloat16
i32 = jnp.int32

FAR_FIRST = (4, 3, 5, 2, 6, 1, 7)
FIRST = 12
OFFSETS = (-2, 2, -1, 1)


def ring(d, size):
    return min(d, size - d)


def split(x):
    hi = x.astype(bf16)
    return hi, (x - hi.astype(f32)).astype(bf16)


def lane_block(rows):
    return lax.broadcasted_iota(i32, (rows, 128), 1) // R


def kernel(
    near_src_hbm,
    near_dst_hbm,
    near_count_hbm,
    far_src_hbm,
    far_dst_hbm,
    u_hbm,
    s_hbm,
    a_hbm,
    b_hbm,
    blocks_hbm,
    coupling_hbm,
    bases_hbm,
    transfer_hbm,
    coarse_hbm,
    out,
    near_src,
    near_dst,
    near_count,
    u_in,
    s_in,
    a_ref,
    b_ref,
    blocks,
    far_src_row,
    far_dst_row,
    coupling,
    bases,
    transfer,
    coarse,
    near_at,
    near_to,
    w_coefs,
    w_built,
    w_sent,
    w_came,
    w_own,
    w_far,
    w_sum,
    u_now,
    s_now,
    inverse,
    known,
    u_sum,
    s_sum,
    tab_a,
    tab_o,
    tab_r,
    tab_b,
    tab_f,
    part_f,
    expansion,
    tab_n,
    work_n,
    load_sem,
    coupling_sem,
    a_send,
    a_recv,
    o_send,
    o_recv,
    r_send,
    r_recv,
    f_send,
    f_recv,
    b_send,
    b_recv,
    w_send,
    w_recv,
    n_send,
    n_recv,
):
    st = lax.axis_index("strike")
    dv = lax.axis_index("dev")
    core = lax.rem(st, 2)
    x = lax.div(st, 2)
    z = lax.div(dv, SIDE)
    y = lax.rem(dv, SIDE)
    other = st + 1 - 2 * core
    my_a = y + core * (z - y)
    my_b = z + core * (y - z)
    step_a = 1 + (SIDE - 1) * core
    step_b = SIDE - (SIDE - 1) * core

    def on_a(d):
        return (st, lax.rem(my_a + d, SIDE) * step_a + my_b * step_b)

    def on_b(d):
        return (st, my_a * step_a + lax.rem(my_b + d, SIDE) * step_b)

    def on_other(d):
        return (other, my_a * step_a + lax.rem(my_b + d, SIDE) * step_b)

    def from_other(d):
        return (other, lax.rem(my_a + d, SIDE) * step_a + my_b * step_b)

    def on_xb(dx, d):
        return (lax.rem(x + dx, XS) * 2 + core, my_a * step_a + lax.rem(my_b + d, SIDE) * step_b)

    far_xb = sorted(
        ((dx, d) for dx in range(XS) for d in range(SIDE) if dx or d),
        key=lambda p: -(ring(p[0], XS) + ring(p[1], SIDE)),
    )

    def has(o):
        return (dv + o >= 0) & (dv + o < SIDE * SIDE)

    loads = [
        (u_hbm.at[:, 0], u_in.at[0]),
        (u_hbm.at[:, 1], u_in.at[1]),
        (bases_hbm, bases),
        (transfer_hbm, transfer),
        (near_src_hbm, near_src),
        (near_dst_hbm, near_dst),
        (near_count_hbm, near_count),
        (far_src_hbm, far_src_row),
        (far_dst_hbm, far_dst_row),
        (s_hbm.at[:, 0], s_in.at[0]),
        (s_hbm.at[:, 1], s_in.at[1]),
        (a_hbm, a_ref),
        (b_hbm, b_ref),
        (coarse_hbm, coarse),
        (blocks_hbm.at[0], blocks),
    ]
    loads = [pltpu.make_async_copy(src, dst, load_sem.at[i]) for i, (src, dst) in enumerate(loads)]
    for load in loads[:4]:
        load.start()
    partners = [to(d) for d in FAR_FIRST for to in (on_a, from_other)] + [from_other(0)]
    partners += [on_xb(dx, d) for dx, d in far_xb]
    barrier = pltpu.get_barrier_semaphore()
    for to in partners:
        pl.semaphore_signal(barrier, inc=1, device_id=to)
    n_near = jnp.int32(0)
    for o in OFFSETS:
        n_near = n_near + has(o).astype(i32)

        @pl.when(has(o))
        def _():
            pl.semaphore_signal(barrier, inc=1, device_id=(st, dv + o))

    for r in range(R):
        pltpu.make_async_copy(coupling_hbm.at[0, :, r], coupling.at[r], coupling_sem).start()
    for load in loads[4:]:
        load.start()

    for o in OFFSETS:

        @pl.when(jnp.logical_not(has(o)))
        def _():
            empty = jnp.zeros((STAGES, CL, E, PS), bf16)
            tab_n[:, (o + REACH) * CL : (o + REACH + 1) * CL] = empty

    for load in loads[:4]:
        load.wait()

    for c in range(CL):
        row = lax.broadcasted_iota(i32, (R, 128), 0)
        lane = lax.broadcasted_iota(i32, (R, 128), 1)
        placed = ((lane % R == row) & ((lane // R) % CL == c)).astype(f32)
        right = jnp.concatenate([placed] + [transfer[c]] * 4, axis=1)
        hi, lo = split(
            lax.dot_general(
                bases[c].astype(f32), right, (((0,), (0,)), ((), ())), precision=highest, preferred_element_type=f32
            )
        )
        w_coefs[c * PS : (c + 1) * PS, 0:256] = hi
        w_coefs[c * PS : (c + 1) * PS, 256:384] = lo[:, 128:256]

    for c in range(CL):
        u_now[c] = u_in[c]
    u_sum[...] = jnp.zeros_like(u_sum)
    s_sum[...] = jnp.zeros_like(s_sum)

    def build_far():
        for load in loads[4:9]:
            load.wait()
        pltpu.make_async_copy(coupling, coupling, coupling_sem).wait()
        src = far_src_row[...]
        owner = src >> 1
        its_y, its_z = owner & (SIDE - 1), owner >> 3
        its_a, its_b = its_y + core * (its_z - its_y), its_z + core * (its_y - its_z)
        place = jnp.concatenate([its_b * SIDE + its_a] * 4, axis=1)
        kind = jnp.concatenate([(src & 1) * CL + far_dst_row[...]] * 4, axis=1)
        places = SIDE * SIDE
        chosen = (lax.broadcasted_iota(i32, (places, 128), 0) == place) & (lane_block(places) == kind)
        chosen = jnp.where(chosen, 1.0, 0.0).astype(bf16)
        chosen = jnp.concatenate([chosen, chosen], axis=1)
        quarter = lane_block(NF)

        def rows_of(r4, carry):
            for i in range(4):
                r = r4 * 4 + i
                wide = jnp.concatenate([coupling[r]] * 4, axis=1)
                parts = [split(jnp.where(quarter == j, wide, 0.0)) for j in range(4)]
                right = jnp.concatenate([p[0] for p in parts] + [p[1] for p in parts], axis=0)
                rows = jnp.dot(chosen, right, preferred_element_type=f32)
                at = pl.ds(pl.multiple_of(r * SIDE, SIDE), SIDE)
                w_built[:, at] = rows.reshape(SIDE, SIDE, 128)
            return carry

        lax.fori_loop(0, R // 4, rows_of, 0)
        for b in range(SIDE):
            for a in range(SIDE):
                w_sent[b, a] = w_built[b, pl.ds(a, R, stride=SIDE), :].astype(bf16)
        w_came[my_b] = w_sent[my_b]

        def unpack_own(b, carry):
            unpack(w_sent, b, lambda a, j: w_own.at[pl.ds(pl.multiple_of(b * SIDE * 128 + a * 128 + j * R, R), R)])
            return carry

        lax.fori_loop(0, SIDE, unpack_own, 0)

    def unpack(packed, b, to):
        low = lax.broadcasted_iota(i32, (R, 128), 1) < 64
        for a in range(SIDE):
            block = packed[b, a].astype(f32)
            turned = pltpu.roll(block, 64, 1)
            for j, (here, mask) in enumerate(((block, low), (turned, low), (turned, ~low), (block, ~low))):
                to(a, j)[...] = jnp.where(mask, here, 0.0).astype(bf16)

    def unpack_far():
        wait_blocks(w_came, SIDE - 1, w_recv)

        def column_of(b, carry):
            at = pl.ds(pl.multiple_of(b * 128, 128), 128)
            unpack(w_came, b, lambda a, j: w_far.at[pl.ds(a * 128 + j * R, R), at])
            return carry

        lax.fori_loop(0, SIDE, column_of, 0)

    def prepare():
        for load in loads[9:]:
            load.wait()
        count = near_count[0]
        for k in range(NB):
            src = near_src[0, k]
            at = (lax.div(src, CL) - dv + REACH) * CL + lax.rem(src, CL)
            near_at[k] = jnp.minimum(jnp.maximum(at, 0), (2 * REACH + 1) * CL - 1)
            for c in range(CL):
                near_to[c, k] = jnp.where((near_dst[0, k] == c) & (count > k), 1.0, 0.0).astype(f32)
        for c in range(CL):
            s_now[c] = s_in[c]
            hi, lo = split(
                jnp.dot(
                    coarse[c].reshape(GROUPS * R, R), bases[c].astype(f32), precision=highest, preferred_element_type=f32
                )
            )
            w_sum[0 : GROUPS * R, c * PS : (c + 1) * PS] = hi
            w_sum[GROUPS * R : 2 * GROUPS * R, c * PS : (c + 1) * PS] = lo
        w_sum[2 * GROUPS * R :] = jnp.zeros((128, CL * PS), bf16)
        for c in range(CL):
            at = 2 * GROUPS * R + c * R
            w_sum[at : at + R, c * PS : (c + 1) * PS] = bases[c]

    def near_copy(s, o):
        return pltpu.make_async_remote_copy(
            src_ref=tab_n.at[s, pl.ds(REACH * CL, CL)],
            dst_ref=tab_n.at[s, pl.ds((REACH - o) * CL, CL)],
            send_sem=n_send.at[s, o + REACH],
            recv_sem=n_recv.at[s, REACH - o],
            device_id=(st, dv + o),
        )

    def push(src, dst, send, recv, to):
        pltpu.make_async_remote_copy(
            src_ref=src, dst_ref=dst, send_sem=send, recv_sem=recv, device_id=to
        ).start()

    def wait_blocks(ref, n, sem):
        part = ref.at[pl.ds(0, n)]
        pltpu.make_async_copy(part, part, sem).wait()

    block = lane_block(HALF)

    def begin(s):
        for c in range(CL):
            tab_n[s, REACH * CL + c] = (jnp.exp(u_now[c]) - 1.0).astype(bf16)
        deficit = jnp.concatenate([tab_n[s, REACH * CL + c] for c in range(CL)], axis=1)
        both = jnp.dot(deficit, w_coefs[...], preferred_element_type=f32)
        coefs = jnp.where(block < CL, both[0:HALF, 0:128], both[HALF:E, 0:128])
        shares = both[:, 128:256] + both[:, 256:384]
        share = jnp.where(block == core, shares[0:HALF], 0.0)
        share = jnp.where(block == CL + core, shares[HALF:E], share)
        tab_a[s, my_a, 0:HALF] = coefs.astype(bf16)
        tab_a[s, my_a, HALF:E] = share.astype(bf16)

    def wait_sends(s):
        wait_blocks(tab_a.at[s], SIDE - 1, a_send.at[s])
        wait_blocks(tab_o.at[s], SIDE, o_send.at[s])
        wait_blocks(tab_r.at[s].reshape(XS * SIDE, HALF, 128), XS * SIDE - 1, r_send.at[s])
        for o in OFFSETS:

            @pl.when(has(o))
            def _():
                near_copy(s, o).wait_send()

    def send_coefs():
        tab_b[my_b] = tab_a[0, :, 0:HALF]
        for d in FAR_FIRST:
            push(tab_b.at[my_b], tab_b.at[my_b], b_send, b_recv, on_b(d))

    def send_weights():
        for d in FAR_FIRST:
            push(w_sent.at[lax.rem(my_b + d, SIDE)], w_came.at[my_b], w_send, w_recv, on_b(d))

    def far_first():
        wait_blocks(tab_b, SIDE - 1, b_recv)
        sources = jnp.concatenate([tab_b[b, a] for b in range(SIDE) for a in range(SIDE)], axis=1)
        expansion[...] = jnp.dot(sources, w_own[...], preferred_element_type=f32)

    def far_later(s):
        wait_blocks(tab_f.at[s], SIDE - 1, f_recv.at[s])
        expansion[...] = jnp.sum(tab_f[s].astype(f32), axis=0)

    def send_far(s):
        sources = jnp.concatenate([tab_a[s, i, 0:HALF] for i in range(SIDE)], axis=1)
        parts = jnp.dot(sources, w_far[...], preferred_element_type=f32).astype(bf16)
        for i in range(SIDE):
            part_f[s, i] = parts[:, i * 128 : (i + 1) * 128]
        for d in FAR_FIRST:
            push(part_f.at[s, lax.rem(my_b + d, SIDE)], tab_f.at[s, my_b], f_send.at[s], f_recv.at[s], on_b(d))
        tab_f[s, my_b] = part_f[s, my_b]

    def stage(s, carry):
        mine = tab_a.at[s, my_a]
        share = mine.at[pl.ds(HALF, HALF)]
        for d in FAR_FIRST:
            push(mine, mine, a_send.at[s], a_recv.at[s], on_a(d))
            push(share, tab_o.at[s, my_b], o_send.at[s], o_recv.at[s], on_other(d))
        push(share, tab_o.at[s, my_b], o_send.at[s], o_recv.at[s], on_other(0))
        for o in OFFSETS:

            @pl.when(has(o))
            def _():
                near_copy(s, o).start()

        pl.when(s == 0)(build_far)
        pl.when(s == 0)(prepare)
        pl.when(s == 1)(unpack_far)
        pl.when(s > 0)(lambda: wait_sends(s - 1))

        wait_blocks(tab_a.at[s], SIDE - 1, a_recv.at[s])
        wait_blocks(tab_o.at[s], SIDE, o_recv.at[s])
        row_sum = jnp.sum(tab_a[s, :, HALF:E].astype(f32) + tab_o[s].astype(f32), axis=0)
        tab_r[s, x, my_b] = row_sum.astype(bf16)
        mine = tab_r.at[s, x, my_b]
        for dx, d in far_xb[:FIRST]:
            push(mine, mine, r_send.at[s], r_recv.at[s], on_xb(dx, d))
        pl.when(s == 0)(send_coefs)
        pl.when(s > 0)(lambda: send_far(s))
        for dx, d in far_xb[FIRST:]:
            push(mine, mine, r_send.at[s], r_recv.at[s], on_xb(dx, d))

        pl.when(s == 0)(send_weights)

        for o in OFFSETS:

            @pl.when(has(-o))
            def _():
                near_copy(s, o).wait_recv()

        work_n[...] = tab_n[s]
        near = jnp.zeros((CL * E, PS), f32)
        for k0 in range(0, NB, PIECE):
            lhs = []
            for k in range(k0, k0 + PIECE):
                rows = work_n[near_at[k]]
                lhs.append(
                    jnp.concatenate(
                        [rows * jnp.full((E, PS), near_to[c, k], f32).astype(bf16) for c in range(CL)],
                        axis=0,
                    )
                )
            near = near + jnp.dot(
                jnp.concatenate(lhs, axis=1),
                blocks[k0 : k0 + PIECE].reshape(PIECE * PS, PS),
                preferred_element_type=f32,
            )

        ahead = jnp.where(s == 2, time_step, 0.5 * time_step).astype(f32)
        weight = jnp.where((s == 1) | (s == 2), 2.0, 1.0).astype(f32)
        for c in range(CL):
            velocity = jnp.exp(u_now[c])
            ds = jnp.exp(-s_now[c]) - velocity
            s_sum[c] += weight * ds
            s_now[c] = s_in[c] + ahead * ds
            inverse[c] = 1.0 / (a_ref[c : c + 1] + viscous * velocity)
            known[c] = near[c * E : (c + 1) * E] + b_ref[c : c + 1] * ds

        pl.when(s == 0)(far_first)
        pl.when(s > 0)(lambda: far_later(s))
        halves = jnp.concatenate([expansion[...], pltpu.roll(expansion[...], 64, 1)], axis=0).astype(bf16)
        wait_blocks(tab_r.at[s].reshape(XS * SIDE, HALF, 128), XS * SIDE - 1, r_recv.at[s])
        low = block < CL
        sums = [jnp.sum(tab_r[s, i].astype(f32), axis=0) for i in range(XS)]
        turned = [pltpu.roll(v, 64, 1) for v in sums]
        rows = []
        for half in range(2):
            first, second = (sums, turned) if half == 0 else (turned, sums)
            rows.append(
                jnp.concatenate(
                    [jnp.where(low, first[2 * t], second[2 * t + 1]) for t in range(XS // 2)], axis=1
                )
            )
        groups = jnp.concatenate(rows, axis=0).astype(bf16)
        far = jnp.dot(
            jnp.concatenate([groups, groups, halves], axis=1), w_sum[...], preferred_element_type=f32
        )
        for c in range(CL):
            du = -(known[c] + far[:, c * PS : (c + 1) * PS]) * inverse[c]
            u_now[c] = u_in[c] + ahead * du
            u_sum[c] += weight * du

        pl.when(s < STAGES - 1)(lambda: begin(s + 1))
        return carry

    begin(0)
    pl.semaphore_wait(barrier, len(partners) + n_near)
    lax.fori_loop(0, STAGES, stage, 0)
    wait_sends(STAGES - 1)
    wait_blocks(tab_b, SIDE - 1, b_send)
    wait_blocks(w_came, SIDE - 1, w_send)
    for s in range(1, STAGES):
        wait_blocks(tab_f.at[s], SIDE - 1, f_send.at[s])
    for c in range(CL):
        out[0, :, c] = (time_step / 6.0) * u_sum[c]
        out[1, :, c] = (time_step / 6.0) * s_sum[c]


def per_device(
    log_rate,
    state_log,
    a_coef,
    b_coef,
    near_src,
    near_dst,
    near_count,
    near_blocks,
    far_src,
    far_dst,
    far_coupling,
    cluster_bases,
    transfer,
    coarse_coupling,
):
    vmem = pl.BlockSpec(memory_space=pltpu.VMEM)
    hbm = pl.BlockSpec(memory_space=pl.ANY)
    state = (CL, E, PS)
    dma = pltpu.SemaphoreType.DMA
    step = pl.pallas_call(
        kernel,
        out_shape=jax.ShapeDtypeStruct((2, E, CL, PS), f32),
        in_specs=[hbm] * 14,
        out_specs=vmem,
        scratch_shapes=[
            pltpu.SMEM((1, NB), i32),
            pltpu.SMEM((1, NB), i32),
            pltpu.SMEM((1,), i32),
            pltpu.VMEM(state, f32),
            pltpu.VMEM(state, f32),
            pltpu.VMEM((CL, PS), f32),
            pltpu.VMEM((CL, PS), f32),
            pltpu.VMEM((NB, PS, PS), bf16),
            pltpu.VMEM((1, NF), i32),
            pltpu.VMEM((1, NF), i32),
            pltpu.VMEM((R, NF, R), f32),
            pltpu.VMEM((CL, R, PS), bf16),
            pltpu.VMEM((CL, R, R), f32),
            pltpu.VMEM((CL, GROUPS, R, R), f32),
            pltpu.SMEM((NB,), i32),
            pltpu.SMEM((CL, NB), f32),
            pltpu.VMEM((CL * PS, 384), bf16),
            pltpu.VMEM((SIDE, R * SIDE, 128), f32),
            pltpu.VMEM((SIDE, SIDE, R, 128), bf16),
            pltpu.VMEM((SIDE, SIDE, R, 128), bf16),
            pltpu.VMEM((SIDE * SIDE * 128, 128), bf16),
            pltpu.VMEM((SIDE * 128, SIDE * 128), bf16),
            pltpu.VMEM((2 * GROUPS * R + 128, CL * PS), bf16),
            pltpu.VMEM(state, f32),
            pltpu.VMEM(state, f32),
            pltpu.VMEM(state, f32),
            pltpu.VMEM(state, f32),
            pltpu.VMEM(state, f32),
            pltpu.VMEM(state, f32),
            pltpu.VMEM((STAGES, SIDE, E, 128), bf16),
            pltpu.VMEM((STAGES, SIDE, HALF, 128), bf16),
            pltpu.VMEM((STAGES, XS, SIDE, HALF, 128), bf16),
            pltpu.VMEM((SIDE, SIDE, HALF, 128), bf16),
            pltpu.VMEM((STAGES, SIDE, HALF, 128), bf16),
            pltpu.VMEM((STAGES, SIDE, HALF, 128), bf16),
            pltpu.VMEM((HALF, 128), f32),
            pltpu.VMEM((STAGES, (2 * REACH + 1) * CL, E, PS), bf16),
            pltpu.VMEM(((2 * REACH + 1) * CL, E, PS), bf16),
            dma((15,)),
            dma,
        ]
        + [dma((STAGES,))] * 8
        + [dma] * 4
        + [dma((STAGES, 2 * REACH + 1))] * 2,
        compiler_params=pltpu.CompilerParams(
            collective_id=0, has_side_effects=True, vmem_limit_bytes=56 * 1024 * 1024
        ),
    )(
        near_src,
        near_dst,
        near_count,
        far_src,
        far_dst,
        log_rate,
        state_log,
        a_coef,
        b_coef,
        near_blocks,
        far_coupling,
        cluster_bases,
        transfer,
        coarse_coupling,
    )
    return log_rate + step[0], state_log + step[1]


def solution(mesh):
    cluster = ("strike", "dev")
    state = P(None, cluster, None)
    placed = (
        state,
        state,
        P(cluster, None),
        P(cluster, None),
        P(cluster, None),
        P(cluster, None),
        P(cluster),
        P(cluster, None, None, None),
        P(cluster, None),
        P(cluster, None),
        P(cluster, None, None, None),
        P(cluster, None, None),
        P(cluster, None, None),
        P(cluster, None, None, None),
    )
    return jax.shard_map(
        per_device, mesh=mesh, in_specs=placed, out_specs=(state, state), check_vma=False
    )
```

```python
import jax
import jax.numpy as jnp
from jax import lax
from jax.experimental import pallas as pl
from jax.experimental.pallas import tpu as pltpu
from jax.sharding import PartitionSpec as P

CL = 2
NB = 32
NF = 32
REACH = 2
E = 32
R = 32
PS = 256
SIDE = 8
XS = 4
GROUPS = 8
STAGES = 4
HALF = E // 2
PIECE = 4

time_step = 0.25
viscous = 0.5
highest = lax.Precision.HIGHEST
f32 = jnp.float32
bf16 = jnp.bfloat16
i32 = jnp.int32

FAR_FIRST = (4, 3, 5, 2, 6, 1, 7)
FIRST = 12
OFFSETS = (-2, 2, -1, 1)


def ring(d, size):
    return min(d, size - d)


def split(x):
    hi = x.astype(bf16)
    return hi, (x - hi.astype(f32)).astype(bf16)


def lane_block(rows):
    return lax.broadcasted_iota(i32, (rows, 128), 1) // R


def kernel(
    near_src_hbm,
    near_dst_hbm,
    near_count_hbm,
    far_src_hbm,
    far_dst_hbm,
    u_hbm,
    s_hbm,
    a_hbm,
    b_hbm,
    blocks_hbm,
    coupling_hbm,
    bases_hbm,
    transfer_hbm,
    coarse_hbm,
    out,
    near_src,
    near_dst,
    near_count,
    u_in,
    s_in,
    a_ref,
    b_ref,
    blocks,
    far_src_row,
    far_dst_row,
    coupling,
    bases,
    transfer,
    coarse,
    near_at,
    near_to,
    w_coefs,
    w_built,
    w_sent,
    w_came,
    w_own,
    w_far,
    w_sum,
    u_now,
    s_now,
    inverse,
    known,
    u_sum,
    s_sum,
    tab_a,
    tab_o,
    tab_r,
    tab_b,
    tab_f,
    part_f,
    expansion,
    tab_n,
    work_n,
    load_sem,
    coupling_sem,
    a_send,
    a_recv,
    o_send,
    o_recv,
    r_send,
    r_recv,
    f_send,
    f_recv,
    b_send,
    b_recv,
    w_send,
    w_recv,
    n_send,
    n_recv,
):
    st = lax.axis_index("strike")
    dv = lax.axis_index("dev")
    core = lax.rem(st, 2)
    x = lax.div(st, 2)
    z = lax.div(dv, SIDE)
    y = lax.rem(dv, SIDE)
    other = st + 1 - 2 * core
    my_a = y + core * (z - y)
    my_b = z + core * (y - z)
    step_a = 1 + (SIDE - 1) * core
    step_b = SIDE - (SIDE - 1) * core

    def on_a(d):
        return (st, lax.rem(my_a + d, SIDE) * step_a + my_b * step_b)

    def on_b(d):
        return (st, my_a * step_a + lax.rem(my_b + d, SIDE) * step_b)

    def on_other(d):
        return (other, my_a * step_a + lax.rem(my_b + d, SIDE) * step_b)

    def from_other(d):
        return (other, lax.rem(my_a + d, SIDE) * step_a + my_b * step_b)

    def on_xb(dx, d):
        return (lax.rem(x + dx, XS) * 2 + core, my_a * step_a + lax.rem(my_b + d, SIDE) * step_b)

    far_xb = sorted(
        ((dx, d) for dx in range(XS) for d in range(SIDE) if dx or d),
        key=lambda p: -(ring(p[0], XS) + ring(p[1], SIDE)),
    )

    def has(o):
        return (dv + o >= 0) & (dv + o < SIDE * SIDE)

    partners = [on_xb(dx, d) for dx, d in far_xb]
    partners += [to(d) for d in FAR_FIRST for to in (on_a, from_other)] + [from_other(0)]
    barrier = pltpu.get_barrier_semaphore()
    for to in partners:
        pl.semaphore_signal(barrier, inc=1, device_id=to)
    n_near = jnp.int32(0)
    for o in OFFSETS:
        n_near = n_near + has(o).astype(i32)

        @pl.when(has(o))
        def _():
            pl.semaphore_signal(barrier, inc=1, device_id=(st, dv + o))

    loads = [
        (u_hbm.at[:, 0], u_in.at[0]),
        (u_hbm.at[:, 1], u_in.at[1]),
        (bases_hbm, bases),
        (transfer_hbm, transfer),
        (near_src_hbm, near_src),
        (near_dst_hbm, near_dst),
        (near_count_hbm, near_count),
        (far_src_hbm, far_src_row),
        (far_dst_hbm, far_dst_row),
        (s_hbm.at[:, 0], s_in.at[0]),
        (s_hbm.at[:, 1], s_in.at[1]),
        (a_hbm, a_ref),
        (b_hbm, b_ref),
        (coarse_hbm, coarse),
        (blocks_hbm.at[0], blocks),
    ]
    loads = [pltpu.make_async_copy(src, dst, load_sem.at[i]) for i, (src, dst) in enumerate(loads)]
    for load in loads[:4]:
        load.start()
    for r in range(R):
        pltpu.make_async_copy(coupling_hbm.at[0, :, r], coupling.at[r], coupling_sem).start()
    for load in loads[4:]:
        load.start()

    for o in OFFSETS:

        @pl.when(jnp.logical_not(has(o)))
        def _():
            empty = jnp.zeros((STAGES, CL, E, PS), bf16)
            tab_n[:, (o + REACH) * CL : (o + REACH + 1) * CL] = empty

    for load in loads[:4]:
        load.wait()

    for c in range(CL):
        row = lax.broadcasted_iota(i32, (R, 128), 0)
        lane = lax.broadcasted_iota(i32, (R, 128), 1)
        placed = ((lane % R == row) & ((lane // R) % CL == c)).astype(f32)
        right = jnp.concatenate([placed] + [transfer[c]] * 4, axis=1)
        hi, lo = split(
            lax.dot_general(
                bases[c].astype(f32), right, (((0,), (0,)), ((), ())), precision=highest, preferred_element_type=f32
            )
        )
        w_coefs[c * PS : (c + 1) * PS, 0:256] = hi
        w_coefs[c * PS : (c + 1) * PS, 256:384] = lo[:, 128:256]

    for c in range(CL):
        u_now[c] = u_in[c]
    u_sum[...] = jnp.zeros_like(u_sum)
    s_sum[...] = jnp.zeros_like(s_sum)

    def build_far():
        for load in loads[4:9]:
            load.wait()
        pltpu.make_async_copy(coupling, coupling, coupling_sem).wait()
        src = far_src_row[...]
        owner = src >> 1
        its_y, its_z = owner & (SIDE - 1), owner >> 3
        its_a, its_b = its_y + core * (its_z - its_y), its_z + core * (its_y - its_z)
        place = jnp.concatenate([its_b * SIDE + its_a] * 4, axis=1)
        kind = jnp.concatenate([(src & 1) * CL + far_dst_row[...]] * 4, axis=1)
        places = SIDE * SIDE
        chosen = (lax.broadcasted_iota(i32, (places, 128), 0) == place) & (lane_block(places) == kind)
        chosen = jnp.where(chosen, 1.0, 0.0).astype(bf16)
        chosen = jnp.concatenate([chosen, chosen], axis=1)
        quarter = lane_block(NF)

        def rows_of(r4, carry):
            for i in range(4):
                r = r4 * 4 + i
                wide = jnp.concatenate([coupling[r]] * 4, axis=1)
                parts = [split(jnp.where(quarter == j, wide, 0.0)) for j in range(4)]
                right = jnp.concatenate([p[0] for p in parts] + [p[1] for p in parts], axis=0)
                rows = jnp.dot(chosen, right, preferred_element_type=f32)
                at = pl.ds(pl.multiple_of(r * SIDE, SIDE), SIDE)
                w_built[:, at] = rows.reshape(SIDE, SIDE, 128)
            return carry

        lax.fori_loop(0, R // 4, rows_of, 0)
        for b in range(SIDE):
            for a in range(SIDE):
                w_sent[b, a] = w_built[b, pl.ds(a, R, stride=SIDE), :].astype(bf16)
        w_came[my_b] = w_sent[my_b]

        def unpack_own(b, carry):
            unpack(w_sent, b, lambda a, j: w_own.at[pl.ds(pl.multiple_of(b * SIDE * 128 + a * 128 + j * R, R), R)])
            return carry

        lax.fori_loop(0, SIDE, unpack_own, 0)

    def unpack(packed, b, to):
        low = lax.broadcasted_iota(i32, (R, 128), 1) < 64
        for a in range(SIDE):
            block = packed[b, a].astype(f32)
            turned = pltpu.roll(block, 64, 1)
            for j, (here, mask) in enumerate(((block, low), (turned, low), (turned, ~low), (block, ~low))):
                to(a, j)[...] = jnp.where(mask, here, 0.0).astype(bf16)

    def unpack_far():
        wait_blocks(w_came, SIDE - 1, w_recv)

        def column_of(b, carry):
            at = pl.ds(pl.multiple_of(b * 128, 128), 128)
            unpack(w_came, b, lambda a, j: w_far.at[pl.ds(a * 128 + j * R, R), at])
            return carry

        lax.fori_loop(0, SIDE, column_of, 0)

    def prepare():
        for load in loads[9:]:
            load.wait()
        count = near_count[0]
        for k in range(NB):
            src = near_src[0, k]
            at = (lax.div(src, CL) - dv + REACH) * CL + lax.rem(src, CL)
            near_at[k] = jnp.minimum(jnp.maximum(at, 0), (2 * REACH + 1) * CL - 1)
            for c in range(CL):
                near_to[c, k] = jnp.where((near_dst[0, k] == c) & (count > k), 1.0, 0.0).astype(f32)
        for c in range(CL):
            s_now[c] = s_in[c]
            hi, lo = split(
                jnp.dot(
                    coarse[c].reshape(GROUPS * R, R), bases[c].astype(f32), precision=highest, preferred_element_type=f32
                )
            )
            w_sum[0 : GROUPS * R, c * PS : (c + 1) * PS] = hi
            w_sum[GROUPS * R : 2 * GROUPS * R, c * PS : (c + 1) * PS] = lo
        w_sum[2 * GROUPS * R :] = jnp.zeros((128, CL * PS), bf16)
        for c in range(CL):
            at = 2 * GROUPS * R + c * R
            w_sum[at : at + R, c * PS : (c + 1) * PS] = bases[c]

    def near_copy(s, o):
        return pltpu.make_async_remote_copy(
            src_ref=tab_n.at[s, pl.ds(REACH * CL, CL)],
            dst_ref=tab_n.at[s, pl.ds((REACH - o) * CL, CL)],
            send_sem=n_send.at[s, o + REACH],
            recv_sem=n_recv.at[s, REACH - o],
            device_id=(st, dv + o),
        )

    def push(src, dst, send, recv, to):
        pltpu.make_async_remote_copy(
            src_ref=src, dst_ref=dst, send_sem=send, recv_sem=recv, device_id=to
        ).start()

    def wait_blocks(ref, n, sem):
        part = ref.at[pl.ds(0, n)]
        pltpu.make_async_copy(part, part, sem).wait()

    block = lane_block(HALF)

    def begin(s):
        for c in range(CL):
            tab_n[s, REACH * CL + c] = (jnp.exp(u_now[c]) - 1.0).astype(bf16)
        deficit = jnp.concatenate([tab_n[s, REACH * CL + c] for c in range(CL)], axis=1)
        both = jnp.dot(deficit, w_coefs[...], preferred_element_type=f32)
        coefs = jnp.where(block < CL, both[0:HALF, 0:128], both[HALF:E, 0:128])
        shares = both[:, 128:256] + both[:, 256:384]
        share = jnp.where(block == core, shares[0:HALF], 0.0)
        share = jnp.where(block == CL + core, shares[HALF:E], share)
        tab_a[s, my_a, 0:HALF] = coefs.astype(bf16)
        tab_a[s, my_a, HALF:E] = share.astype(bf16)

    def wait_sends(s):
        wait_blocks(tab_a.at[s], SIDE - 1, a_send.at[s])
        wait_blocks(tab_o.at[s], SIDE, o_send.at[s])
        wait_blocks(tab_r.at[s].reshape(XS * SIDE, HALF, 128), XS * SIDE - 1, r_send.at[s])
        for o in OFFSETS:

            @pl.when(has(o))
            def _():
                near_copy(s, o).wait_send()

    def send_first():
        tab_b[my_b] = tab_a[0, :, 0:HALF]
        for d in FAR_FIRST:
            push(tab_b.at[my_b], tab_b.at[my_b], b_send, b_recv, on_b(d))
        for d in FAR_FIRST:
            push(w_sent.at[lax.rem(my_b + d, SIDE)], w_came.at[my_b], w_send, w_recv, on_b(d))

    def far_first():
        wait_blocks(tab_b, SIDE - 1, b_recv)
        sources = jnp.concatenate([tab_b[b, a] for b in range(SIDE) for a in range(SIDE)], axis=1)
        expansion[...] = jnp.dot(sources, w_own[...], preferred_element_type=f32)

    def far_later(s):
        wait_blocks(tab_f.at[s], SIDE - 1, f_recv.at[s])
        expansion[...] = jnp.sum(tab_f[s].astype(f32), axis=0)

    def send_far(s):
        sources = jnp.concatenate([tab_a[s, i, 0:HALF] for i in range(SIDE)], axis=1)
        parts = jnp.dot(sources, w_far[...], preferred_element_type=f32).astype(bf16)
        for i in range(SIDE):
            part_f[s, i] = parts[:, i * 128 : (i + 1) * 128]
        for d in FAR_FIRST:
            push(part_f.at[s, lax.rem(my_b + d, SIDE)], tab_f.at[s, my_b], f_send.at[s], f_recv.at[s], on_b(d))
        tab_f[s, my_b] = part_f[s, my_b]

    def stage(s, carry):
        mine = tab_a.at[s, my_a]
        share = mine.at[pl.ds(HALF, HALF)]
        for d in FAR_FIRST:
            push(mine, mine, a_send.at[s], a_recv.at[s], on_a(d))
            push(share, tab_o.at[s, my_b], o_send.at[s], o_recv.at[s], on_other(d))
        push(share, tab_o.at[s, my_b], o_send.at[s], o_recv.at[s], on_other(0))
        for o in OFFSETS:

            @pl.when(has(o))
            def _():
                near_copy(s, o).start()

        pl.when(s == 0)(build_far)
        pl.when(s == 0)(prepare)
        pl.when(s == 1)(unpack_far)
        pl.when(s > 0)(lambda: wait_sends(s - 1))

        wait_blocks(tab_a.at[s], SIDE - 1, a_recv.at[s])
        wait_blocks(tab_o.at[s], SIDE, o_recv.at[s])
        row_sum = jnp.sum(tab_a[s, :, HALF:E].astype(f32) + tab_o[s].astype(f32), axis=0)
        tab_r[s, x, my_b] = row_sum.astype(bf16)
        mine = tab_r.at[s, x, my_b]
        for dx, d in far_xb[:FIRST]:
            push(mine, mine, r_send.at[s], r_recv.at[s], on_xb(dx, d))
        pl.when(s > 0)(lambda: send_far(s))
        for dx, d in far_xb[FIRST:]:
            push(mine, mine, r_send.at[s], r_recv.at[s], on_xb(dx, d))

        pl.when(s == 0)(send_first)

        for o in OFFSETS:

            @pl.when(has(-o))
            def _():
                near_copy(s, o).wait_recv()

        work_n[...] = tab_n[s]
        near = jnp.zeros((CL * E, PS), f32)
        for k0 in range(0, NB, PIECE):
            lhs = []
            for k in range(k0, k0 + PIECE):
                rows = work_n[near_at[k]]
                lhs.append(
                    jnp.concatenate(
                        [rows * jnp.full((E, PS), near_to[c, k], f32).astype(bf16) for c in range(CL)],
                        axis=0,
                    )
                )
            near = near + jnp.dot(
                jnp.concatenate(lhs, axis=1),
                blocks[k0 : k0 + PIECE].reshape(PIECE * PS, PS),
                preferred_element_type=f32,
            )

        ahead = jnp.where(s == 2, time_step, 0.5 * time_step).astype(f32)
        weight = jnp.where((s == 1) | (s == 2), 2.0, 1.0).astype(f32)
        for c in range(CL):
            velocity = jnp.exp(u_now[c])
            ds = jnp.exp(-s_now[c]) - velocity
            s_sum[c] += weight * ds
            s_now[c] = s_in[c] + ahead * ds
            inverse[c] = 1.0 / (a_ref[c : c + 1] + viscous * velocity)
            known[c] = near[c * E : (c + 1) * E] + b_ref[c : c + 1] * ds

        pl.when(s == 0)(far_first)
        pl.when(s > 0)(lambda: far_later(s))
        halves = jnp.concatenate([expansion[...], pltpu.roll(expansion[...], 64, 1)], axis=0).astype(bf16)
        wait_blocks(tab_r.at[s].reshape(XS * SIDE, HALF, 128), XS * SIDE - 1, r_recv.at[s])
        low = block < CL
        sums = [jnp.sum(tab_r[s, i].astype(f32), axis=0) for i in range(XS)]
        turned = [pltpu.roll(v, 64, 1) for v in sums]
        rows = []
        for half in range(2):
            first, second = (sums, turned) if half == 0 else (turned, sums)
            rows.append(
                jnp.concatenate(
                    [jnp.where(low, first[2 * t], second[2 * t + 1]) for t in range(XS // 2)], axis=1
                )
            )
        groups = jnp.concatenate(rows, axis=0).astype(bf16)
        far = jnp.dot(
            jnp.concatenate([groups, groups, halves], axis=1), w_sum[...], preferred_element_type=f32
        )
        for c in range(CL):
            du = -(known[c] + far[:, c * PS : (c + 1) * PS]) * inverse[c]
            u_now[c] = u_in[c] + ahead * du
            u_sum[c] += weight * du

        pl.when(s < STAGES - 1)(lambda: begin(s + 1))
        return carry

    begin(0)
    pl.semaphore_wait(barrier, len(partners) + n_near)
    lax.fori_loop(0, STAGES, stage, 0)
    wait_sends(STAGES - 1)
    wait_blocks(tab_b, SIDE - 1, b_send)
    wait_blocks(w_came, SIDE - 1, w_send)
    for s in range(1, STAGES):
        wait_blocks(tab_f.at[s], SIDE - 1, f_send.at[s])
    for c in range(CL):
        out[0, :, c] = (time_step / 6.0) * u_sum[c]
        out[1, :, c] = (time_step / 6.0) * s_sum[c]


def per_device(
    log_rate,
    state_log,
    a_coef,
    b_coef,
    near_src,
    near_dst,
    near_count,
    near_blocks,
    far_src,
    far_dst,
    far_coupling,
    cluster_bases,
    transfer,
    coarse_coupling,
):
    vmem = pl.BlockSpec(memory_space=pltpu.VMEM)
    hbm = pl.BlockSpec(memory_space=pl.ANY)
    state = (CL, E, PS)
    dma = pltpu.SemaphoreType.DMA
    step = pl.pallas_call(
        kernel,
        out_shape=jax.ShapeDtypeStruct((2, E, CL, PS), f32),
        in_specs=[hbm] * 14,
        out_specs=vmem,
        scratch_shapes=[
            pltpu.SMEM((1, NB), i32),
            pltpu.SMEM((1, NB), i32),
            pltpu.SMEM((1,), i32),
            pltpu.VMEM(state, f32),
            pltpu.VMEM(state, f32),
            pltpu.VMEM((CL, PS), f32),
            pltpu.VMEM((CL, PS), f32),
            pltpu.VMEM((NB, PS, PS), bf16),
            pltpu.VMEM((1, NF), i32),
            pltpu.VMEM((1, NF), i32),
            pltpu.VMEM((R, NF, R), f32),
            pltpu.VMEM((CL, R, PS), bf16),
            pltpu.VMEM((CL, R, R), f32),
            pltpu.VMEM((CL, GROUPS, R, R), f32),
            pltpu.SMEM((NB,), i32),
            pltpu.SMEM((CL, NB), f32),
            pltpu.VMEM((CL * PS, 384), bf16),
            pltpu.VMEM((SIDE, R * SIDE, 128), f32),
            pltpu.VMEM((SIDE, SIDE, R, 128), bf16),
            pltpu.VMEM((SIDE, SIDE, R, 128), bf16),
            pltpu.VMEM((SIDE * SIDE * 128, 128), bf16),
            pltpu.VMEM((SIDE * 128, SIDE * 128), bf16),
            pltpu.VMEM((2 * GROUPS * R + 128, CL * PS), bf16),
            pltpu.VMEM(state, f32),
            pltpu.VMEM(state, f32),
            pltpu.VMEM(state, f32),
            pltpu.VMEM(state, f32),
            pltpu.VMEM(state, f32),
            pltpu.VMEM(state, f32),
            pltpu.VMEM((STAGES, SIDE, E, 128), bf16),
            pltpu.VMEM((STAGES, SIDE, HALF, 128), bf16),
            pltpu.VMEM((STAGES, XS, SIDE, HALF, 128), bf16),
            pltpu.VMEM((SIDE, SIDE, HALF, 128), bf16),
            pltpu.VMEM((STAGES, SIDE, HALF, 128), bf16),
            pltpu.VMEM((STAGES, SIDE, HALF, 128), bf16),
            pltpu.VMEM((HALF, 128), f32),
            pltpu.VMEM((STAGES, (2 * REACH + 1) * CL, E, PS), bf16),
            pltpu.VMEM(((2 * REACH + 1) * CL, E, PS), bf16),
            dma((15,)),
            dma,
        ]
        + [dma((STAGES,))] * 8
        + [dma] * 4
        + [dma((STAGES, 2 * REACH + 1))] * 2,
        compiler_params=pltpu.CompilerParams(
            collective_id=0, has_side_effects=True, vmem_limit_bytes=56 * 1024 * 1024
        ),
    )(
        near_src,
        near_dst,
        near_count,
        far_src,
        far_dst,
        log_rate,
        state_log,
        a_coef,
        b_coef,
        near_blocks,
        far_coupling,
        cluster_bases,
        transfer,
        coarse_coupling,
    )
    return log_rate + step[0], state_log + step[1]


def solution(mesh):
    cluster = ("strike", "dev")
    state = P(None, cluster, None)
    placed = (
        state,
        state,
        P(cluster, None),
        P(cluster, None),
        P(cluster, None),
        P(cluster, None),
        P(cluster),
        P(cluster, None, None, None),
        P(cluster, None),
        P(cluster, None),
        P(cluster, None, None, None),
        P(cluster, None, None),
        P(cluster, None, None),
        P(cluster, None, None, None),
    )
    return jax.shard_map(
        per_device, mesh=mesh, in_specs=placed, out_specs=(state, state), check_vma=False
    )
```
